512 devices in a mesh: branch: 16 (over y_lo, z), seq: 32 (over x, y_hi, core).
Axes of the slice: x: 4, y: 8 (y_hi: 4, y_lo: 2; y = y_hi * 2 + y_lo), z: 8, core: 2. Of those that a mesh axis runs over, the one named last changes fastest.
Arguments:
- queries: bfloat16 [64, 4096], P('branch', 'seq'), may hold values from -16 to 16
- row_branch: int32 [64], replicated, may hold values from 0 to 15, as said below
- suffix_len: int32 [64], P('branch'), may hold values from 1 to 2048, as said below
- common_keys: bfloat16 [131072, 512], P(('branch', 'seq')), may hold values from -16 to 16
- common_values: bfloat16 [131072, 512], P(('branch', 'seq')), may hold values from -6 to 6
- branch_keys: bfloat16 [16, 16384, 512], P('branch', 'seq'), may hold values from -6 to 6
- branch_values: bfloat16 [16, 16384, 512], P('branch', 'seq'), may hold values from -6 to 6
- suffix_keys: bfloat16 [64, 2048, 512], P('branch', 'seq'), may hold values from -6 to 6
- suffix_values: bfloat16 [64, 2048, 512], P('branch', 'seq'), may hold values from -6 to 6
Outputs:
- attended: bfloat16 [64, 4096], P('branch', 'seq')
The draws below stay inside these ranges and needn't reach their ends.
Inputs may be any that keep to these rules, and one draw needn't show every extreme that they name: `row_branch`: each of the 16 branches is named by exactly 4 rows. `suffix_len`: some row has all 2048 suffix tokens live.
All inputs are finite; a program needn't handle non-finite values.
Results may differ from the reference program's by a relative error of at most 0.0029.
Values may be sent and summed in bfloat16 or wider, within the bound.
No kernel may reach another device: no remote copies, remote signals or barrier semaphores. Data moves between devices by JAX's collectives and lax.ppermute only.
A program may use at most 64 MiB of HBM per device.

```python
import math
import jax
import jax.numpy as jnp
from jax import lax

HEADS = 32
KV_HEADS = 4
HEAD_DIM = 128
ROW_GRP = 4
COM_DEV = 256
SUF_DEV = 64
ROWS = 64
COMMON_TOK = 131072
BRANCH_TOK = 16384
SUF_LEN = 2048
N_BRANCH = 16
N_SEQ = 32


def draw_queries(key, part):
    key = jax.random.fold_in(key, 1)
    key_base = jax.random.fold_in(key, 0)
    row_count = ROW_GRP * N_BRANCH
    full_shape = (row_count, HEADS * HEAD_DIM)
    values = 3.0 * jnp.clip(jax.random.normal(key_base, full_shape, jnp.float32), -4.0, 4.0)
    return values.astype(jnp.bfloat16)


def draw_common_keys(key, part):
    key = jax.random.fold_in(key, 2)
    key_base = jax.random.fold_in(key, 0)
    key_count = COM_DEV * N_BRANCH * N_SEQ
    full_shape = (key_count, KV_HEADS * HEAD_DIM)
    values = jnp.clip(jax.random.normal(key_base, full_shape, jnp.float32), -4.0, 4.0)
    return values.astype(jnp.bfloat16)


def draw_row_branch(key, part):
    key = jax.random.fold_in(key, 5)
    row_count = ROW_GRP * N_BRANCH
    return (jax.random.permutation(key, row_count) // ROW_GRP).astype(jnp.int32)


def draw_suffix_len(key, part):
    key = jax.random.fold_in(key, 3)
    key_len, key_row = jax.random.split(key)
    row_count = ROW_GRP * N_BRANCH
    longest = SUF_DEV * N_SEQ
    lengths = jax.random.randint(key_len, (row_count,), 1, longest + 1)
    picked = jax.random.randint(key_row, (), 0, row_count)
    return lengths.at[picked].set(longest).astype(jnp.int32)


def steps_of(key, dims, cuts, smallest, high):
    def one(axis_at, shards_of):
        heights = jax.random.uniform(jax.random.fold_in(jax.random.fold_in(key, 6), axis_at), (shards_of,), jnp.float32, smallest / len(cuts), high / len(cuts))
        return jnp.repeat(jnp.exp(heights), dims[axis_at] // shards_of).reshape((-1,) + (1,) * (len(dims) - axis_at - 1))

    loudness = one(*cuts[0])
    for cut in cuts[1:]:
        loudness = loudness * one(*cut)
    return loudness


def normal_values(own_key, extent, spread, reach, pieces=(), held_as=jnp.bfloat16):
    result = spread * jax.random.normal(own_key, extent, jnp.float32)
    if pieces:
        result = result * steps_of(own_key, extent, pieces, -0.22, 0.18)
    return jnp.clip(result, -reach, reach).astype(held_as)


def setup_inputs(seed: int = 0) -> dict:
    splits = jax.random.split(jax.random.key(seed), 10)
    queries = draw_queries(jax.random.fold_in(splits[9], 71), 0)
    row_branch = draw_row_branch(jax.random.fold_in(splits[9], 71), 0)
    suffix_len = draw_suffix_len(jax.random.fold_in(splits[9], 71), 0)
    common_keys = draw_common_keys(jax.random.fold_in(splits[9], 71), 0)
    common_values = normal_values(splits[4], (COMMON_TOK, KV_HEADS * HEAD_DIM), 1.0, 6.0, ((0, 512),))
    branch_keys = normal_values(splits[5], (N_BRANCH, BRANCH_TOK, KV_HEADS * HEAD_DIM), 1.0, 6.0, ((0, 16), (1, 32)))
    branch_values = normal_values(splits[6], (N_BRANCH, BRANCH_TOK, KV_HEADS * HEAD_DIM), 1.0, 6.0, ((0, 16), (1, 32)))
    suffix_keys = normal_values(splits[7], (ROWS, SUF_LEN, KV_HEADS * HEAD_DIM), 1.0, 6.0, ((0, 16), (1, 32)))
    suffix_values = normal_values(splits[8], (ROWS, SUF_LEN, KV_HEADS * HEAD_DIM), 1.0, 6.0, ((0, 16), (1, 32)))
    return dict(queries=queries, row_branch=row_branch, suffix_len=suffix_len, common_keys=common_keys, common_values=common_values, branch_keys=branch_keys, branch_values=branch_values, suffix_keys=suffix_keys, suffix_values=suffix_values)


def reference(queries, row_branch, suffix_len, common_keys, common_values, branch_keys, branch_values, suffix_keys, suffix_values):
    per_kv = HEADS // KV_HEADS
    score_scale = 1.0 / math.sqrt(HEAD_DIM)
    row_count = queries.shape[0]
    own_rows = row_count // N_BRANCH
    query_all = queries.astype(jnp.float32).reshape(row_count, KV_HEADS, per_kv, HEAD_DIM)
    blocks = N_BRANCH * N_SEQ // 8
    key_common = common_keys.reshape(blocks, -1, KV_HEADS, HEAD_DIM)
    val_common = common_values.reshape(blocks, -1, KV_HEADS, HEAD_DIM)

    def common_scores(key_block):
        return jnp.einsum('rkgd,tkd->rkgt', query_all, key_block.astype(jnp.float32)) * score_scale

    def block_max(running, key_block):
        return (jnp.maximum(running, lax.optimization_barrier(jnp.max(common_scores(key_block), axis=-1))), None)
    initial = jnp.full((row_count, KV_HEADS, per_kv), -jnp.inf, jnp.float32)
    common_max, _ = lax.scan(block_max, initial, key_common)
    row_order = jnp.argsort(row_branch, stable=True).astype(jnp.int32)
    branch_q = query_all[row_order].reshape(N_BRANCH, own_rows, KV_HEADS, per_kv, HEAD_DIM)
    key_branch = branch_keys.astype(jnp.float32).reshape(N_BRANCH, -1, KV_HEADS, HEAD_DIM)
    val_branch = branch_values.astype(jnp.float32).reshape(N_BRANCH, -1, KV_HEADS, HEAD_DIM)
    branch_scores = jnp.einsum('brkgd,btkd->brkgt', branch_q, key_branch) * score_scale
    branch_max = lax.optimization_barrier(jnp.max(branch_scores, axis=-1)).reshape(row_count, KV_HEADS, per_kv)
    branch_max = jnp.zeros_like(common_max).at[row_order].set(branch_max)
    key_suffix = suffix_keys.astype(jnp.float32).reshape(row_count, -1, KV_HEADS, HEAD_DIM)
    val_suffix = suffix_values.astype(jnp.float32).reshape(row_count, -1, KV_HEADS, HEAD_DIM)
    suffix_scores = jnp.einsum('rkgd,rtkd->rkgt', query_all, key_suffix) * score_scale
    positions = jnp.arange(key_suffix.shape[1], dtype=jnp.int32)
    is_live = positions[None, :] < suffix_len[:, None]
    suffix_masked = jnp.where(is_live[:, None, None, :], suffix_scores, -jnp.inf)
    suffix_max = lax.optimization_barrier(jnp.max(suffix_masked, axis=-1))
    row_max = jnp.maximum(jnp.maximum(common_max, branch_max), suffix_max)

    def block_sums(running, pair):
        key_block, val_block = pair
        weights = jnp.exp(common_scores(key_block) - row_max[..., None])
        rounded = lax.optimization_barrier(weights.astype(jnp.bfloat16))
        numer = jnp.einsum('rkgt,tkd->rkgd', rounded.astype(jnp.float32), val_block.astype(jnp.float32))
        return ((running[0] + numer, running[1] + lax.optimization_barrier(jnp.sum(weights, axis=-1))), None)
    zero_out = jnp.zeros((row_count, KV_HEADS, per_kv, HEAD_DIM), jnp.float32)
    zero_sum = jnp.zeros((row_count, KV_HEADS, per_kv), jnp.float32)
    (common_out, common_sum), _ = lax.scan(block_sums, (zero_out, zero_sum), (key_common, val_common))
    branch_rmax = row_max[row_order].reshape(N_BRANCH, own_rows, KV_HEADS, per_kv)
    branch_w = jnp.exp(branch_scores - branch_rmax[..., None])
    branch_r = lax.optimization_barrier(branch_w.astype(jnp.bfloat16))
    branch_out = jnp.einsum('brkgt,btkd->brkgd', branch_r.astype(jnp.float32), val_branch)
    branch_out = zero_out.at[row_order].set(branch_out.reshape(row_count, KV_HEADS, per_kv, HEAD_DIM))
    branch_sum = zero_sum.at[row_order].set(lax.optimization_barrier(jnp.sum(branch_w, axis=-1)).reshape(row_count, KV_HEADS, per_kv))
    suffix_w = jnp.where(is_live[:, None, None, :], jnp.exp(suffix_masked - row_max[..., None]), 0.0)
    suffix_r = lax.optimization_barrier(suffix_w.astype(jnp.bfloat16))
    suffix_out = jnp.einsum('rkgt,rtkd->rkgd', suffix_r.astype(jnp.float32), val_suffix)
    suffix_sum = lax.optimization_barrier(jnp.sum(suffix_w, axis=-1))
    numer_all = common_out + branch_out + suffix_out
    total_all = common_sum + branch_sum + suffix_sum
    attended = numer_all / total_all[..., None]
    return attended.reshape(row_count, HEADS * HEAD_DIM).astype(jnp.bfloat16)
```

```python
import functools
import math

import jax
import jax.numpy as jnp
from jax import lax
from jax.experimental import pallas as pl
from jax.experimental.pallas import tpu as pltpu
from jax.sharding import Mesh
from jax.sharding import PartitionSpec as P

HEADS = 32
KV_HEADS = 4
GROUP = HEADS // KV_HEADS
HEAD_DIM = 128
N_X, N_YHI, N_CORE, N_YLO, N_Z = 4, 4, 2, 2, 8
PLANE = ("z", "yhi", "ylo", "core")
PEERS = N_Z * N_YHI * N_YLO * N_CORE
ROWS = 64
OWN = 4
COM, BRA, SUF = 256, 512, 64
KEYS = COM + BRA + OWN * SUF
LINES = PEERS * OWN
PICKED = OWN * GROUP
CHUNK = OWN + 1
LOW = -1e30
F32 = jnp.float32
BF16 = jnp.bfloat16
SCALE = math.log2(math.e) / math.sqrt(HEAD_DIM)
VMEM = pl.BlockSpec(memory_space=pltpu.VMEM)
SMEM = pl.BlockSpec(memory_space=pltpu.SMEM)
ANY = pl.BlockSpec(memory_space=pl.ANY)
VMEM_LIMIT = 48 * 1024 * 1024


def pack_kernel(place, ck, cv, bk, bv, sk, sv, *rest):
    outs, sem = rest[:N_X], rest[N_X]
    x = place[1]
    copies = []
    for i in range(N_X):
        head = lax.rem(x + i, N_X)
        cols = pl.ds(pl.multiple_of(head * HEAD_DIM, HEAD_DIM), HEAD_DIM)
        at = 0
        for n, (src, count) in enumerate(
            ((ck, COM), (bk, BRA), (sk, OWN * SUF), (cv, COM), (bv, BRA), (sv, OWN * SUF))
        ):
            copy = pltpu.make_async_copy(src.at[:, cols], outs[i].at[pl.ds(at, count)], sem.at[i, n])
            copy.start()
            copies.append(copy)
            at += count
    for copy in copies:
        copy.wait()


def attend(q, keys, values, mask=None):
    scores = []
    for i, key in enumerate(keys):
        s = lax.dot_general(q, key, (((1,), (1,)), ((), ())), preferred_element_type=F32) * SCALE
        scores.append(s if mask is None else jnp.where(mask[i], s, LOW))
    top = jnp.max(functools.reduce(jnp.maximum, scores), axis=1, keepdims=True)
    total = out = None
    for i, (s, value) in enumerate(zip(scores, values)):
        w = jnp.exp2(s - top)
        if mask is not None:
            w = jnp.where(mask[i], w, 0.0)
        o = jnp.dot(w.astype(BF16), value, preferred_element_type=F32)
        total = w if total is None else total + w
        out = o if out is None else out + o
    return out, top, jnp.sum(total, axis=1, keepdims=True)


def attend_kernel(place, row_branch, suffix_len, q_ref, kv0, kv1, kv2, kv3, out_ref, pick):
    branch, x, yhi, core = place[0], place[1], place[2], place[3]
    kvs = (kv0, kv1, kv2, kv3)

    def blocks(at, count):
        return [kv[pl.ds(at, count)] for kv in kvs], [kv[pl.ds(KEYS + at, count)] for kv in kvs]

    found = jnp.int32(0)
    for i in range(ROWS):
        pick[found] = jnp.int32(i)
        found = found + (row_branch[i] == branch).astype(jnp.int32)

    q = q_ref[...]
    out, top, total = attend(q, *blocks(0, COM))

    def lines(shape, axis):
        at = lax.broadcasted_iota(jnp.int32, shape, axis)
        slot = (at >> 3) & (OWN - 1)
        row = jnp.zeros(shape, jnp.int32)
        for j in range(OWN):
            row = jnp.where(slot == j, jnp.where(at < PICKED, pick[j], branch * OWN + j), row)
        ylo, z, r = row >> 5, (row >> 2) & 7, row & 3
        yh, co = (at >> 1) & 3, at & 1
        return (((z * N_YHI + yh) * N_YLO + ylo) * N_CORE + co) * OWN + r

    shape = (2 * PICKED, LINES)
    select = lax.broadcasted_iota(jnp.int32, shape, 1) == lines(shape, 0)
    q_sel = jnp.dot(select.astype(F32).astype(BF16), q, preferred_element_type=F32).astype(BF16)
    b_out, b_top, b_total = attend(q_sel[:PICKED], *blocks(COM, BRA))

    shape = (PICKED, OWN * SUF)
    q_row = lax.broadcasted_iota(jnp.int32, shape, 0) >> 3
    slot = lax.broadcasted_iota(jnp.int32, shape, 1)
    k_row, slot = slot >> 6, slot & (SUF - 1)
    live = jnp.zeros(shape, jnp.int32)
    for j in range(OWN):
        live = jnp.where(k_row == j, suffix_len[j], live)
    mask = []
    for i in range(N_X):
        from_x = lax.rem(x + N_X - i, N_X)
        first = ((from_x * N_YHI + yhi) * N_CORE + core) * SUF
        mask.append((q_row == k_row) & (slot + first < live))
    s_out, s_top, s_total = attend(q_sel[PICKED:], *blocks(COM + BRA, OWN * SUF), mask)

    square = (2 * PICKED, 2 * PICKED)
    eye = lax.broadcasted_iota(jnp.int32, square, 0) == lax.broadcasted_iota(jnp.int32, square, 1)

    def across(a, b):
        col = jnp.broadcast_to(jnp.concatenate([a, b], axis=0), square)
        return jnp.sum(jnp.where(eye, col, 0.0), axis=0, keepdims=True)

    shape = (LINES, 2 * PICKED)
    place_of = lax.broadcasted_iota(jnp.int32, shape, 0) == lines(shape, 1)
    p_top = jnp.where(place_of, jnp.broadcast_to(across(b_top, s_top), shape), LOW)
    high = jnp.maximum(top, jnp.max(p_top, axis=1, keepdims=True))
    weight = jnp.where(place_of, jnp.exp2(p_top - high), 0.0)
    scale = jnp.exp2(top - high)
    parts = jnp.concatenate([b_out, s_out], axis=0)
    out = out * scale + jnp.dot(
        weight, parts, precision=lax.Precision.HIGHEST, preferred_element_type=F32
    )
    total = total * scale + jnp.sum(weight * across(b_total, s_total), axis=1, keepdims=True)

    shape = (LINES, HEAD_DIM)
    lane = lax.broadcasted_iota(jnp.int32, shape, 1)
    r = lax.broadcasted_iota(jnp.int32, shape, 0) & (OWN - 1)
    stat = jnp.where(lane == r, high, 0.0) + jnp.where(lane == r + OWN, total, 0.0)
    stat = sum(pltpu.roll(stat, i, 0) for i in range(1, OWN)) + stat
    for c in range(PEERS):
        out_ref[pl.ds(c * CHUNK, OWN)] = out[c * OWN : (c + 1) * OWN]
        out_ref[pl.ds(c * CHUNK + OWN, 1)] = stat[(c + 1) * OWN - 1 : (c + 1) * OWN]


def merge_kernel(parts, out):
    stat = parts[pl.ds(OWN, PEERS, stride=CHUNK), :]
    high = jnp.max(stat, axis=0, keepdims=True)
    weight = jnp.exp2(jnp.minimum(stat - high, 0.0))
    total = jnp.sum(pltpu.roll(weight, OWN, 1) * stat, axis=0, keepdims=True)
    rows = []
    for r in range(OWN):
        part = parts[pl.ds(r, PEERS, stride=CHUNK), :]
        got = jnp.sum(part * weight[:, r : r + 1], axis=0, keepdims=True)
        rows.append(got / total[:, OWN + r : OWN + r + 1])
    out[...] = jnp.concatenate(rows, axis=0).astype(BF16)


def call(kernel, outs, specs, scratch=()):
    return pl.pallas_call(
        kernel,
        out_shape=outs,
        in_specs=specs,
        out_specs=VMEM,
        scratch_shapes=scratch,
        compiler_params=pltpu.CompilerParams(vmem_limit_bytes=VMEM_LIMIT),
    )


def turn(value, axis, step):
    size = lax.axis_size(axis)
    return lax.ppermute(value, axis, [(i, (i + step) % size) for i in range(size)])


def local(
    queries,
    row_branch,
    suffix_len,
    common_keys,
    common_values,
    branch_keys,
    branch_values,
    suffix_keys,
    suffix_values,
):
    ylo, z, x, yhi, core = (lax.axis_index(a) for a in ("ylo", "z", "x", "yhi", "core"))
    place = jnp.stack([ylo * N_Z + z, x, yhi, core]).astype(jnp.int32)
    width = KV_HEADS * HEAD_DIM
    flat = [
        a.reshape(-1, width)
        for a in (common_keys, common_values, branch_keys, branch_values, suffix_keys, suffix_values)
    ]
    packed = pl.pallas_call(
        pack_kernel,
        out_shape=[jax.ShapeDtypeStruct((2 * KEYS, HEAD_DIM), BF16)] * N_X,
        in_specs=[SMEM] + [ANY] * 6,
        out_specs=[ANY] * N_X,
        scratch_shapes=[pltpu.SemaphoreType.DMA((N_X, 6))],
    )(place, *flat)
    kvs = [packed[0]] + [turn(packed[i], "x", i) for i in range(1, N_X)]

    q = jnp.broadcast_to(queries[None], (PEERS, OWN, HEAD_DIM))
    q = lax.all_to_all(q, PLANE, split_axis=0, concat_axis=0, tiled=True)
    q = q.reshape(LINES, HEAD_DIM)
    parts = call(
        attend_kernel,
        jax.ShapeDtypeStruct((PEERS * CHUNK, HEAD_DIM), F32),
        [SMEM] * 3 + [VMEM] * 5,
        [pltpu.SMEM((8,), jnp.int32)],
    )(place, row_branch, suffix_len, q, *kvs)
    parts = parts.reshape(PEERS * CHUNK, 1, HEAD_DIM)
    parts = lax.all_to_all(parts, PLANE, split_axis=0, concat_axis=0, tiled=True)
    parts = parts.reshape(PEERS * CHUNK, HEAD_DIM)
    return call(merge_kernel, jax.ShapeDtypeStruct((OWN, HEAD_DIM), BF16), [VMEM])(parts)


def solution(mesh):
    axes = ("ylo", "z", "x", "yhi", "core")
    fine = Mesh(mesh.devices.reshape(N_YLO, N_Z, N_X, N_YHI, N_CORE), axes)
    branch, seq = ("ylo", "z"), ("x", "yhi", "core")
    return jax.shard_map(
        local,
        mesh=fine,
        in_specs=(
            P(branch, seq),
            P(),
            P(branch),
            P(branch + seq, None),
            P(branch + seq, None),
            P(branch, seq, None),
            P(branch, seq, None),
            P(branch, seq, None),
            P(branch, seq, None),
        ),
        out_specs=P(branch, seq),
        check_vma=False,
    )
```

```python
import functools
import math

import jax
import jax.numpy as jnp
from jax import lax
from jax.experimental import pallas as pl
from jax.experimental.pallas import tpu as pltpu
from jax.sharding import Mesh
from jax.sharding import PartitionSpec as P

HEADS = 32
KV_HEADS = 4
GROUP = HEADS // KV_HEADS
HEAD_DIM = 128
N_X, N_YHI, N_CORE, N_YLO, N_Z = 4, 4, 2, 2, 8
PLANE = ("z", "yhi", "ylo", "core")
PEERS = N_Z * N_YHI * N_YLO * N_CORE
ROWS = 64
OWN = 4
COM, BRA, SUF = 256, 512, 64
KEYS = COM + BRA + OWN * SUF
LINES = PEERS * OWN
PICKED = OWN * GROUP
CHUNK = OWN + 1
LOW = -1e30
F32 = jnp.float32
BF16 = jnp.bfloat16
SCALE = math.log2(math.e) / math.sqrt(HEAD_DIM)
VMEM = pl.BlockSpec(memory_space=pltpu.VMEM)
ANY = pl.BlockSpec(memory_space=pl.ANY)
VMEM_LIMIT = 48 * 1024 * 1024


def pack_kernel(row_branch, suffix_len, ck, cv, bk, bv, sk, sv, *rest):
    outs, info = rest[:N_X], rest[N_X]
    held, branch_of, live, pick, sem = rest[N_X + 1 :]
    x = lax.axis_index("x")
    branch = lax.axis_index("ylo") * N_Z + lax.axis_index("z")
    small = [
        pltpu.make_async_copy(row_branch, branch_of, sem.at[6]),
        pltpu.make_async_copy(suffix_len, live, sem.at[7]),
    ]
    copies, at = [], 0
    for n, (src, count) in enumerate(
        ((ck, COM), (bk, BRA), (sk, OWN * SUF), (cv, COM), (bv, BRA), (sv, OWN * SUF))
    ):
        rows = pl.ds(at, count)
        copies.append((pltpu.make_async_copy(src, held.at[rows], sem.at[n]), rows))
        at += count
    for copy in small:
        copy.start()
    for copy, _ in copies:
        copy.start()
    for copy in small:
        copy.wait()
    found = jnp.int32(0)
    for i in range(ROWS):
        pick[found] = jnp.int32(i)
        found = found + (branch_of[i] == branch).astype(jnp.int32)
    row = lax.broadcasted_iota(jnp.int32, info.shape, 0)
    words = jnp.zeros(info.shape, jnp.int32)
    for j in range(OWN):
        words = jnp.where(row == j, pick[j], jnp.where(row == OWN + j, live[j], words))
    info[...] = words
    for copy, rows in copies:
        copy.wait()
        for i in range(N_X):
            head = lax.rem(x + i, N_X)
            outs[i][rows] = held[rows, pl.ds(pl.multiple_of(head * HEAD_DIM, HEAD_DIM), HEAD_DIM)]


def attend(q, keys, values, mask=None):
    scores = []
    for i, key in enumerate(keys):
        s = lax.dot_general(q, key, (((1,), (1,)), ((), ())), preferred_element_type=F32) * SCALE
        scores.append(s if mask is None else jnp.where(mask[i], s, LOW))
    top = jnp.max(functools.reduce(jnp.maximum, scores), axis=1, keepdims=True)
    total = out = None
    for i, (s, value) in enumerate(zip(scores, values)):
        w = jnp.exp2(s - top)
        if mask is not None:
            w = jnp.where(mask[i], w, 0.0)
        o = jnp.dot(w.astype(BF16), value, preferred_element_type=F32)
        total = w if total is None else total + w
        out = o if out is None else out + o
    return out, top, jnp.sum(total, axis=1, keepdims=True)


def attend_kernel(info, q_ref, kv0, kv1, kv2, kv3, out_ref):
    x, yhi, core = (lax.axis_index(a) for a in ("x", "yhi", "core"))
    branch = lax.axis_index("ylo") * N_Z + lax.axis_index("z")
    kvs = (kv0, kv1, kv2, kv3)

    def blocks(at, count):
        return [kv[pl.ds(at, count)] for kv in kvs], [kv[pl.ds(KEYS + at, count)] for kv in kvs]

    def word(j, shape):
        return jnp.broadcast_to(info[j : j + 1, 0:1], shape)

    q = q_ref[...]
    out, top, total = attend(q, *blocks(0, COM))

    def lines(shape, axis):
        at = lax.broadcasted_iota(jnp.int32, shape, axis)
        slot = (at >> 3) & (OWN - 1)
        row = jnp.zeros(shape, jnp.int32)
        for j in range(OWN):
            row = jnp.where(slot == j, jnp.where(at < PICKED, word(j, shape), branch * OWN + j), row)
        ylo, z, r = row >> 5, (row >> 2) & 7, row & 3
        yh, co = (at >> 1) & 3, at & 1
        return (((z * N_YHI + yh) * N_YLO + ylo) * N_CORE + co) * OWN + r

    shape = (2 * PICKED, LINES)
    select = lax.broadcasted_iota(jnp.int32, shape, 1) == lines(shape, 0)
    q_sel = jnp.dot(select.astype(F32).astype(BF16), q, preferred_element_type=F32).astype(BF16)
    b_out, b_top, b_total = attend(q_sel[:PICKED], *blocks(COM, BRA))

    shape = (PICKED, OWN * SUF)
    q_row = lax.broadcasted_iota(jnp.int32, shape, 0) >> 3
    slot = lax.broadcasted_iota(jnp.int32, shape, 1)
    k_row, slot = slot >> 6, slot & (SUF - 1)
    live = jnp.zeros(shape, jnp.int32)
    for j in range(OWN):
        live = jnp.where(k_row == j, word(OWN + j, shape), live)
    mask = []
    for i in range(N_X):
        from_x = lax.rem(x + N_X - i, N_X)
        first = ((from_x * N_YHI + yhi) * N_CORE + core) * SUF
        mask.append((q_row == k_row) & (slot + first < live))
    s_out, s_top, s_total = attend(q_sel[PICKED:], *blocks(COM + BRA, OWN * SUF), mask)

    square = (2 * PICKED, 2 * PICKED)
    eye = lax.broadcasted_iota(jnp.int32, square, 0) == lax.broadcasted_iota(jnp.int32, square, 1)

    def across(a, b):
        col = jnp.broadcast_to(jnp.concatenate([a, b], axis=0), square)
        return jnp.sum(jnp.where(eye, col, 0.0), axis=0, keepdims=True)

    shape = (LINES, 2 * PICKED)
    place_of = lax.broadcasted_iota(jnp.int32, shape, 0) == lines(shape, 1)
    p_top = jnp.where(place_of, jnp.broadcast_to(across(b_top, s_top), shape), LOW)
    high = jnp.maximum(top, jnp.max(p_top, axis=1, keepdims=True))
    weight = jnp.where(place_of, jnp.exp2(p_top - high), 0.0)
    scale = jnp.exp2(top - high)
    parts = jnp.concatenate([b_out, s_out], axis=0)
    out = out * scale + jnp.dot(
        weight, parts, precision=lax.Precision.HIGHEST, preferred_element_type=F32
    )
    total = total * scale + jnp.sum(weight * across(b_total, s_total), axis=1, keepdims=True)

    shape = (LINES, HEAD_DIM)
    lane = lax.broadcasted_iota(jnp.int32, shape, 1)
    r = lax.broadcasted_iota(jnp.int32, shape, 0) & (OWN - 1)
    stat = jnp.where(lane == r, high, 0.0) + jnp.where(lane == r + OWN, total, 0.0)
    stat = sum(pltpu.roll(stat, i, 0) for i in range(1, OWN)) + stat
    for c in range(PEERS):
        out_ref[pl.ds(c * CHUNK, OWN)] = out[c * OWN : (c + 1) * OWN]
        out_ref[pl.ds(c * CHUNK + OWN, 1)] = stat[(c + 1) * OWN - 1 : (c + 1) * OWN]


def merge_kernel(parts, out):
    stat = parts[pl.ds(OWN, PEERS, stride=CHUNK), :]
    high = jnp.max(stat, axis=0, keepdims=True)
    weight = jnp.exp2(jnp.minimum(stat - high, 0.0))
    total = jnp.sum(pltpu.roll(weight, OWN, 1) * stat, axis=0, keepdims=True)
    rows = []
    for r in range(OWN):
        part = parts[pl.ds(r, PEERS, stride=CHUNK), :]
        got = jnp.sum(part * weight[:, r : r + 1], axis=0, keepdims=True)
        rows.append(got / total[:, OWN + r : OWN + r + 1])
    out[...] = jnp.concatenate(rows, axis=0).astype(BF16)


def call(kernel, outs, specs, scratch=()):
    return pl.pallas_call(
        kernel,
        out_shape=outs,
        in_specs=specs,
        out_specs=jax.tree.map(lambda _: VMEM, outs),
        scratch_shapes=scratch,
        compiler_params=pltpu.CompilerParams(vmem_limit_bytes=VMEM_LIMIT),
    )


def turn(value, axis, step):
    size = lax.axis_size(axis)
    return lax.ppermute(value, axis, [(i, (i + step) % size) for i in range(size)])


def local(
    queries,
    row_branch,
    suffix_len,
    common_keys,
    common_values,
    branch_keys,
    branch_values,
    suffix_keys,
    suffix_values,
):
    width = KV_HEADS * HEAD_DIM
    flat = [
        a.reshape(-1, width)
        for a in (common_keys, common_values, branch_keys, branch_values, suffix_keys, suffix_values)
    ]
    *packed, info = call(
        pack_kernel,
        [jax.ShapeDtypeStruct((2 * KEYS, HEAD_DIM), BF16)] * N_X
        + [jax.ShapeDtypeStruct((2 * OWN, HEAD_DIM), jnp.int32)],
        [ANY] * 8,
        [
            pltpu.VMEM((2 * KEYS, width), BF16),
            pltpu.SMEM((ROWS,), jnp.int32),
            pltpu.SMEM((OWN,), jnp.int32),
            pltpu.SMEM((2 * OWN,), jnp.int32),
            pltpu.SemaphoreType.DMA((8,)),
        ],
    )(row_branch, suffix_len, *flat)
    kvs = [packed[0]] + [turn(packed[i], "x", i) for i in range(1, N_X)]

    q = jnp.broadcast_to(queries[None], (PEERS, OWN, HEAD_DIM))
    q = lax.all_to_all(q, PLANE, split_axis=0, concat_axis=0, tiled=True)
    q = q.reshape(LINES, HEAD_DIM)
    parts = call(
        attend_kernel,
        jax.ShapeDtypeStruct((PEERS * CHUNK, HEAD_DIM), F32),
        [VMEM] * 6,
    )(info, q, *kvs)
    parts = parts.reshape(PEERS * CHUNK, 1, HEAD_DIM)
    parts = lax.all_to_all(parts, PLANE, split_axis=0, concat_axis=0, tiled=True)
    parts = parts.reshape(PEERS * CHUNK, HEAD_DIM)
    return call(merge_kernel, jax.ShapeDtypeStruct((OWN, HEAD_DIM), BF16), [VMEM])(parts)


def solution(mesh):
    axes = ("ylo", "z", "x", "yhi", "core")
    fine = Mesh(mesh.devices.reshape(N_YLO, N_Z, N_X, N_YHI, N_CORE), axes)
    branch, seq = ("ylo", "z"), ("x", "yhi", "core")
    return jax.shard_map(
        local,
        mesh=fine,
        in_specs=(
            P(branch, seq),
            P(),
            P(branch),
            P(branch + seq, None),
            P(branch + seq, None),
            P(branch, seq, None),
            P(branch, seq, None),
            P(branch, seq, None),
            P(branch, seq, None),
        ),
        out_specs=P(branch, seq),
        check_vma=False,
    )
```

```python
import functools
import math

import jax
import jax.numpy as jnp
from jax import lax
from jax.experimental import pallas as pl
from jax.experimental.pallas import tpu as pltpu
from jax.sharding import Mesh
from jax.sharding import PartitionSpec as P

HEADS = 32
KV_HEADS = 4
GROUP = HEADS // KV_HEADS
HEAD_DIM = 128
N_X, N_YHI, N_CORE, N_YLO, N_Z = 4, 4, 2, 2, 8
PLANE = ("z", "yhi", "ylo", "core")
PEERS = N_Z * N_YHI * N_YLO * N_CORE
ROWS = 64
OWN = 4
COM, BRA, SUF = 256, 512, 64
KEYS = COM + BRA + OWN * SUF
LINES = PEERS * OWN
PICKED = OWN * GROUP
CHUNK = OWN + 1
LOW = -1e30
F32 = jnp.float32
BF16 = jnp.bfloat16
SCALE = math.log2(math.e) / math.sqrt(HEAD_DIM)
VMEM = pl.BlockSpec(memory_space=pltpu.VMEM)
HBM = pl.BlockSpec(memory_space=pltpu.HBM)
VMEM_LIMIT = 48 * 1024 * 1024
PACK_LIMIT = 57 * 1024 * 1024


def pack_kernel(row_branch, suffix_len, ck, cv, bk, bv, sk, sv, *rest):
    outs, info = rest[:N_X], rest[N_X]
    held, blocks, branch_of, live, pick, sem, out_sem = rest[N_X + 1 :]
    x = lax.axis_index("x")
    branch = lax.axis_index("ylo") * N_Z + lax.axis_index("z")
    small = [
        pltpu.make_async_copy(row_branch, branch_of, sem.at[6]),
        pltpu.make_async_copy(suffix_len, live, sem.at[7]),
    ]
    copies, at = [], 0
    for n, (src, count) in enumerate(
        ((ck, COM), (bk, BRA), (sk, OWN * SUF), (cv, COM), (bv, BRA), (sv, OWN * SUF))
    ):
        rows = pl.ds(at, count)
        copies.append((pltpu.make_async_copy(src, held.at[rows], sem.at[n]), rows))
        at += count
    for copy, _ in copies:
        copy.start()
    for copy in small:
        copy.start()
    sent = []
    for n, (copy, rows) in enumerate(copies):
        copy.wait()
        for i in (1, 3, 2, 0):
            head = lax.rem(x + i, N_X)
            cols = pl.ds(pl.multiple_of(head * HEAD_DIM, HEAD_DIM), HEAD_DIM)
            blocks[i, rows] = held[rows, cols]
            out = pltpu.make_async_copy(blocks.at[i, rows], outs[i].at[rows], out_sem.at[i, n])
            out.start()
            sent.append(out)
    for copy in small:
        copy.wait()
    found = jnp.int32(0)
    for i in range(ROWS):
        pick[found] = jnp.int32(i)
        found = found + (branch_of[i] == branch).astype(jnp.int32)
    row = lax.broadcasted_iota(jnp.int32, info.shape, 0)
    words = jnp.zeros(info.shape, jnp.int32)
    for j in range(OWN):
        words = jnp.where(row == j, pick[j], jnp.where(row == OWN + j, live[j], words))
    info[...] = words
    for out in sent:
        out.wait()


def attend(q, keys, values, mask=None, before=None):
    scores = []
    for i, key in enumerate(keys):
        s = lax.dot_general(q, key, (((1,), (1,)), ((), ())), preferred_element_type=F32) * SCALE
        scores.append(s if mask is None else jnp.where(mask[i], s, LOW))
    top = jnp.max(functools.reduce(jnp.maximum, scores), axis=1, keepdims=True)
    if before is not None:
        top = jnp.maximum(top, before[1])
    total = out = None
    for i, (s, value) in enumerate(zip(scores, values)):
        w = jnp.exp2(s - top)
        if mask is not None:
            w = jnp.where(mask[i], w, 0.0)
        o = jnp.dot(w.astype(BF16), value, preferred_element_type=F32)
        total = w if total is None else total + w
        out = o if out is None else out + o
    total = jnp.sum(total, axis=1, keepdims=True)
    if before is not None:
        scale = jnp.exp2(before[1] - top)
        out, total = out + before[0] * scale, total + before[2] * scale
    return out, top, total


def attend_blocks(info, q, q_sel, kvs, steps, before):
    x, yhi, core = (lax.axis_index(a) for a in ("x", "yhi", "core"))

    def blocks(at, count):
        return [kv[pl.ds(at, count)] for kv in kvs], [kv[pl.ds(KEYS + at, count)] for kv in kvs]

    common = attend(q, *blocks(0, COM), before=before[0])
    branch = attend(q_sel[:PICKED], *blocks(COM, BRA), before=before[1])
    shape = (PICKED, OWN * SUF)
    q_row = lax.broadcasted_iota(jnp.int32, shape, 0) >> 3
    slot = lax.broadcasted_iota(jnp.int32, shape, 1)
    k_row, slot = slot >> 6, slot & (SUF - 1)
    live = jnp.zeros(shape, jnp.int32)
    for j in range(OWN):
        live = jnp.where(k_row == j, word(info, OWN + j, shape), live)
    mask = []
    for i in steps:
        first = ((lax.rem(x + N_X - i, N_X) * N_YHI + yhi) * N_CORE + core) * SUF
        mask.append((q_row == k_row) & (slot + first < live))
    suffix = attend(q_sel[PICKED:], *blocks(COM + BRA, OWN * SUF), mask=mask, before=before[2])
    return common, branch, suffix


def word(info, j, shape):
    return jnp.broadcast_to(info[j : j + 1, 0:1], shape)


def picked_lines(info, shape, axis):
    branch = lax.axis_index("ylo") * N_Z + lax.axis_index("z")
    at = lax.broadcasted_iota(jnp.int32, shape, axis)
    slot = (at >> 3) & (OWN - 1)
    row = jnp.zeros(shape, jnp.int32)
    for j in range(OWN):
        row = jnp.where(slot == j, jnp.where(at < PICKED, word(info, j, shape), branch * OWN + j), row)
    ylo, z, r = row >> 5, (row >> 2) & 7, row & 3
    yhi, core = (at >> 1) & 3, at & 1
    return (((z * N_YHI + yhi) * N_YLO + ylo) * N_CORE + core) * OWN + r


PART_LINES = ((0, LINES), (LINES, PICKED), (LINES + PICKED, PICKED))
ALL_LINES = LINES + 2 * PICKED


def own_kernel(info, q_ref, kv, out_ref, stat_ref, sel_ref):
    q = q_ref[...]
    shape = (2 * PICKED, LINES)
    select = lax.broadcasted_iota(jnp.int32, shape, 1) == picked_lines(info, shape, 0)
    q_sel = jnp.dot(select.astype(F32).astype(BF16), q, preferred_element_type=F32).astype(BF16)
    sel_ref[...] = q_sel
    parts = attend_blocks(info, q, q_sel, [kv], [0], [None] * 3)
    for (at, count), (out, top, total) in zip(PART_LINES, parts):
        lane = lax.broadcasted_iota(jnp.int32, (count, HEAD_DIM), 1)
        out_ref[pl.ds(at, count)] = out
        stat_ref[pl.ds(at, count)] = jnp.where(lane == 0, top, total)


def attend_kernel(info, q_ref, sel_ref, own_out, own_stat, kv1, kv2, kv3, out_ref):
    before = []
    for at, count in PART_LINES:
        stat = own_stat[pl.ds(at, count)]
        before.append((own_out[pl.ds(at, count)], stat[:, 0:1], stat[:, 1:2]))
    (out, top, total), (b_out, b_top, b_total), (s_out, s_top, s_total) = attend_blocks(
        info, q_ref[...], sel_ref[...], [kv1, kv2, kv3], [1, 2, 3], before
    )

    square = (2 * PICKED, 2 * PICKED)
    eye = lax.broadcasted_iota(jnp.int32, square, 0) == lax.broadcasted_iota(jnp.int32, square, 1)

    def across(a, b):
        col = jnp.broadcast_to(jnp.concatenate([a, b], axis=0), square)
        return jnp.sum(jnp.where(eye, col, 0.0), axis=0, keepdims=True)

    shape = (LINES, 2 * PICKED)
    place_of = lax.broadcasted_iota(jnp.int32, shape, 0) == picked_lines(info, shape, 1)
    p_top = jnp.where(place_of, jnp.broadcast_to(across(b_top, s_top), shape), LOW)
    high = jnp.maximum(top, jnp.max(p_top, axis=1, keepdims=True))
    weight = jnp.where(place_of, jnp.exp2(p_top - high), 0.0)
    scale = jnp.exp2(top - high)
    parts = jnp.concatenate([b_out, s_out], axis=0)
    out = out * scale + jnp.dot(
        weight, parts, precision=lax.Precision.HIGHEST, preferred_element_type=F32
    )
    total = total * scale + jnp.sum(weight * across(b_total, s_total), axis=1, keepdims=True)

    shape = (LINES, HEAD_DIM)
    lane = lax.broadcasted_iota(jnp.int32, shape, 1)
    r = lax.broadcasted_iota(jnp.int32, shape, 0) & (OWN - 1)
    stat = jnp.where(lane == r, high, 0.0) + jnp.where(lane == r + OWN, total, 0.0)
    stat = sum(pltpu.roll(stat, i, 0) for i in range(1, OWN)) + stat
    for c in range(PEERS):
        out_ref[pl.ds(c * CHUNK, OWN)] = out[c * OWN : (c + 1) * OWN]
        out_ref[pl.ds(c * CHUNK + OWN, 1)] = stat[(c + 1) * OWN - 1 : (c + 1) * OWN]


def merge_kernel(parts, out):
    stat = parts[pl.ds(OWN, PEERS, stride=CHUNK), :]
    high = jnp.max(stat, axis=0, keepdims=True)
    weight = jnp.exp2(jnp.minimum(stat - high, 0.0))
    total = jnp.sum(pltpu.roll(weight, OWN, 1) * stat, axis=0, keepdims=True)
    rows = []
    for r in range(OWN):
        part = parts[pl.ds(r, PEERS, stride=CHUNK), :]
        got = jnp.sum(part * weight[:, r : r + 1], axis=0, keepdims=True)
        rows.append(got / total[:, OWN + r : OWN + r + 1])
    out[...] = jnp.concatenate(rows, axis=0).astype(BF16)


def call(kernel, outs, specs, scratch=(), out_specs=None, limit=VMEM_LIMIT):
    return pl.pallas_call(
        kernel,
        out_shape=outs,
        in_specs=specs,
        out_specs=out_specs or jax.tree.map(lambda _: VMEM, outs),
        scratch_shapes=scratch,
        compiler_params=pltpu.CompilerParams(vmem_limit_bytes=limit),
    )


def turn(value, axis, step):
    size = lax.axis_size(axis)
    return lax.ppermute(value, axis, [(i, (i + step) % size) for i in range(size)])


def local(
    queries,
    row_branch,
    suffix_len,
    common_keys,
    common_values,
    branch_keys,
    branch_values,
    suffix_keys,
    suffix_values,
):
    width = KV_HEADS * HEAD_DIM
    flat = [
        a.reshape(-1, width)
        for a in (common_keys, common_values, branch_keys, branch_values, suffix_keys, suffix_values)
    ]
    *packed, info = call(
        pack_kernel,
        [jax.ShapeDtypeStruct((2 * KEYS, HEAD_DIM), BF16)] * N_X
        + [jax.ShapeDtypeStruct((2 * OWN, HEAD_DIM), jnp.int32)],
        [HBM] * 8,
        [
            pltpu.VMEM((2 * KEYS, width), BF16),
            pltpu.VMEM((N_X, 2 * KEYS, HEAD_DIM), BF16),
            pltpu.SMEM((ROWS,), jnp.int32),
            pltpu.SMEM((OWN,), jnp.int32),
            pltpu.SMEM((2 * OWN,), jnp.int32),
            pltpu.SemaphoreType.DMA((8,)),
            pltpu.SemaphoreType.DMA((N_X, 6)),
        ],
        [HBM] * N_X + [VMEM],
        PACK_LIMIT,
    )(row_branch, suffix_len, *flat)
    kvs = {i: turn(packed[i], "x", i) for i in (1, 3, 2)}
    kvs = [kvs[i] for i in range(1, N_X)]

    q = jnp.broadcast_to(queries[None], (PEERS, OWN, HEAD_DIM))
    q = lax.all_to_all(q, PLANE, split_axis=0, concat_axis=0, tiled=True)
    q = q.reshape(LINES, HEAD_DIM)
    own_out, own_stat, sel = call(
        own_kernel,
        [
            jax.ShapeDtypeStruct((ALL_LINES, HEAD_DIM), F32),
            jax.ShapeDtypeStruct((ALL_LINES, HEAD_DIM), F32),
            jax.ShapeDtypeStruct((2 * PICKED, HEAD_DIM), BF16),
        ],
        [VMEM] * 3,
    )(info, q, packed[0])
    parts = call(
        attend_kernel, jax.ShapeDtypeStruct((PEERS * CHUNK, HEAD_DIM), F32), [VMEM] * 8
    )(info, q, sel, own_out, own_stat, *kvs)
    parts = parts.reshape(PEERS * CHUNK, 1, HEAD_DIM)
    parts = lax.all_to_all(parts, PLANE, split_axis=0, concat_axis=0, tiled=True)
    parts = parts.reshape(PEERS * CHUNK, HEAD_DIM)
    return call(merge_kernel, jax.ShapeDtypeStruct((OWN, HEAD_DIM), BF16), [VMEM])(parts)


def solution(mesh):
    axes = ("ylo", "z", "x", "yhi", "core")
    fine = Mesh(mesh.devices.reshape(N_YLO, N_Z, N_X, N_YHI, N_CORE), axes)
    branch, seq = ("ylo", "z"), ("x", "yhi", "core")
    return jax.shard_map(
        local,
        mesh=fine,
        in_specs=(
            P(branch, seq),
            P(),
            P(branch),
            P(branch + seq, None),
            P(branch + seq, None),
            P(branch, seq, None),
            P(branch, seq, None),
            P(branch, seq, None),
            P(branch, seq, None),
        ),
        out_specs=P(branch, seq),
        check_vma=False,
    )
```

```python
import functools
import math

import jax
import jax.numpy as jnp
from jax import lax
from jax.experimental import pallas as pl
from jax.experimental.pallas import tpu as pltpu
from jax.sharding import Mesh
from jax.sharding import PartitionSpec as P

HEADS = 32
KV_HEADS = 4
GROUP = HEADS // KV_HEADS
HEAD_DIM = 128
N_X, N_YHI, N_CORE, N_YLO, N_Z = 4, 4, 2, 2, 8
PLANE = ("z", "yhi", "ylo", "core")
PEERS = N_Z * N_YHI * N_YLO * N_CORE
ROWS = 64
OWN = 4
COM, BRA, SUF = 256, 512, 64
KEYS = COM + BRA + OWN * SUF
LINES = PEERS * OWN
PICKED = OWN * GROUP
INFO = 16
OWN_ROOM = 1 << 16
CHUNK = OWN + 1
LOW = -1e30
F32 = jnp.float32
BF16 = jnp.bfloat16
SCALE = math.log2(math.e) / math.sqrt(HEAD_DIM)
VMEM = pl.BlockSpec(memory_space=pltpu.VMEM)
HBM = pl.BlockSpec(memory_space=pltpu.HBM)
VMEM_LIMIT = 48 * 1024 * 1024
PACK_LIMIT = 57 * 1024 * 1024


def pack_kernel(row_branch, suffix_len, ck, cv, bk, bv, sk, sv, *rest):
    outs = rest[:N_X]
    held, blocks, info, branch_of, live, pick, sem, out_sem = rest[N_X:]
    x = lax.axis_index("x")
    branch = lax.axis_index("ylo") * N_Z + lax.axis_index("z")
    small = [
        pltpu.make_async_copy(row_branch, branch_of, sem.at[6]),
        pltpu.make_async_copy(suffix_len, live, sem.at[7]),
    ]
    copies, at = [], 0
    for n, (src, count) in enumerate(
        ((ck, COM), (bk, BRA), (sk, OWN * SUF), (cv, COM), (bv, BRA), (sv, OWN * SUF))
    ):
        rows = pl.ds(at, count)
        copies.append((pltpu.make_async_copy(src, held.at[rows], sem.at[n]), rows))
        at += count
    for copy in (*small, *(copy for copy, _ in copies)):
        copy.start()
    for copy in small:
        copy.wait()
    found = jnp.int32(0)
    for i in range(ROWS):
        pick[found] = jnp.int32(i)
        found = found + (branch_of[i] == branch).astype(jnp.int32)
    row = lax.broadcasted_iota(jnp.int32, info.shape, 0)
    words = jnp.zeros(info.shape, jnp.int32)
    for j in range(OWN):
        words = jnp.where(row == j, pick[j], words)
        words = jnp.where(row == OWN + j, live[j] >> 4, words)
        words = jnp.where(row == 2 * OWN + j, live[j] & 15, words)
    info[...] = words.astype(F32).astype(BF16)
    sent = [pltpu.make_async_copy(info, outs[0].at[pl.ds(2 * KEYS, INFO)], out_sem.at[0, 6])]
    sent[0].start()
    for n, (copy, rows) in enumerate(copies):
        copy.wait()
        for i in (1, 3, 2, 0):
            head = lax.rem(x + i, N_X)
            cols = pl.ds(pl.multiple_of(head * HEAD_DIM, HEAD_DIM), HEAD_DIM)
            blocks[i, rows] = held[rows, cols]
            out = pltpu.make_async_copy(blocks.at[i, rows], outs[i].at[rows], out_sem.at[i, n])
            out.start()
            sent.append(out)
    for out in sent:
        out.wait()


def score(q, key, mask=None):
    s = lax.dot_general(q, key, (((1,), (1,)), ((), ())), preferred_element_type=F32) * SCALE
    return s if mask is None else jnp.where(mask, s, LOW)


def weigh(scores, values, masks=None):
    top = jnp.max(functools.reduce(jnp.maximum, scores), axis=1, keepdims=True)
    total = out = None
    for i, (s, value) in enumerate(zip(scores, values)):
        w = jnp.exp2(s - top)
        if masks is not None:
            w = jnp.where(masks[i], w, 0.0)
        o = jnp.dot(w.astype(BF16), value, preferred_element_type=F32)
        total = w if total is None else total + w
        out = o if out is None else out + o
    return out, top, jnp.sum(total, axis=1, keepdims=True)


def picked_lines(picks, shape, axis):
    branch = lax.axis_index("ylo") * N_Z + lax.axis_index("z")
    at = lax.broadcasted_iota(jnp.int32, shape, axis)
    slot = (at >> 3) & (OWN - 1)
    row = branch * OWN + slot
    for j in range(OWN):
        row = jnp.where(at >> 3 == j, jnp.broadcast_to(picks[j], shape), row)
    ylo, z, r = row >> 5, (row >> 2) & 7, row & 3
    yhi, core = (at >> 1) & 3, at & 1
    return (((z * N_YHI + yhi) * N_YLO + ylo) * N_CORE + core) * OWN + r


def attend_kernel(own_hbm, q_ref, kv1, kv2, kv3, out_ref, own, sem):
    x, yhi, core = (lax.axis_index(a) for a in ("x", "yhi", "core"))
    load = pltpu.make_async_copy(own_hbm.at[pl.ds(0, 2 * KEYS + INFO)], own, sem)
    load.start()
    kvs = [kv1, kv2, kv3, own]
    sources = [lax.rem(x + N_X - i, N_X) for i in (1, 2, 3, 0)]

    def key(kv, at, count):
        return kv[pl.ds(at, count)]

    def values(at, count):
        return [kv[pl.ds(KEYS + at, count)] for kv in kvs]

    q = q_ref[...]
    scores = [score(q, key(kv, 0, COM)) for kv in kvs[:-1]]
    load.wait()
    scores.append(score(q, key(own, 0, COM)))
    out, top, total = weigh(scores, values(0, COM))

    info = own[pl.ds(2 * KEYS, INFO)].astype(F32).astype(jnp.int32)
    words = [info[j : j + 1, 0:1] for j in range(3 * OWN)]
    picks = words[:OWN]
    lives = [16 * words[OWN + j] + words[2 * OWN + j] for j in range(OWN)]
    shape = (2 * PICKED, LINES)
    select = lax.broadcasted_iota(jnp.int32, shape, 1) == picked_lines(picks, shape, 0)
    q_sel = jnp.dot(select.astype(F32).astype(BF16), q, preferred_element_type=F32).astype(BF16)
    scores = [score(q_sel[:PICKED], key(kv, COM, BRA)) for kv in kvs]
    b_out, b_top, b_total = weigh(scores, values(COM, BRA))

    shape = (PICKED, OWN * SUF)
    q_row = lax.broadcasted_iota(jnp.int32, shape, 0) >> 3
    slot = lax.broadcasted_iota(jnp.int32, shape, 1)
    k_row, slot = slot >> 6, slot & (SUF - 1)
    live = jnp.zeros(shape, jnp.int32)
    for j in range(OWN):
        live = jnp.where(k_row == j, jnp.broadcast_to(lives[j], shape), live)
    masks = []
    for source in sources:
        first = ((source * N_YHI + yhi) * N_CORE + core) * SUF
        masks.append((q_row == k_row) & (slot + first < live))
    suffix = (COM + BRA, OWN * SUF)
    scores = [score(q_sel[PICKED:], key(kv, *suffix), mask) for kv, mask in zip(kvs, masks)]
    s_out, s_top, s_total = weigh(scores, values(*suffix), masks)

    square = (2 * PICKED, 2 * PICKED)
    eye = lax.broadcasted_iota(jnp.int32, square, 0) == lax.broadcasted_iota(jnp.int32, square, 1)

    def across(a, b):
        col = jnp.broadcast_to(jnp.concatenate([a, b], axis=0), square)
        return jnp.sum(jnp.where(eye, col, 0.0), axis=0, keepdims=True)

    shape = (LINES, 2 * PICKED)
    place_of = lax.broadcasted_iota(jnp.int32, shape, 0) == picked_lines(picks, shape, 1)
    p_top = jnp.where(place_of, jnp.broadcast_to(across(b_top, s_top), shape), LOW)
    high = jnp.maximum(top, jnp.max(p_top, axis=1, keepdims=True))
    weight = jnp.where(place_of, jnp.exp2(p_top - high), 0.0)
    scale = jnp.exp2(top - high)
    parts = jnp.concatenate([b_out, s_out], axis=0)
    out = out * scale + jnp.dot(
        weight, parts, precision=lax.Precision.HIGHEST, preferred_element_type=F32
    )
    total = total * scale + jnp.sum(weight * across(b_total, s_total), axis=1, keepdims=True)

    shape = (LINES, HEAD_DIM)
    lane = lax.broadcasted_iota(jnp.int32, shape, 1)
    r = lax.broadcasted_iota(jnp.int32, shape, 0) & (OWN - 1)
    stat = jnp.where(lane == r, high, 0.0) + jnp.where(lane == r + OWN, total, 0.0)
    stat = sum(pltpu.roll(stat, i, 0) for i in range(1, OWN)) + stat
    for c in range(PEERS):
        out_ref[pl.ds(c * CHUNK, OWN)] = out[c * OWN : (c + 1) * OWN]
        out_ref[pl.ds(c * CHUNK + OWN, 1)] = stat[(c + 1) * OWN - 1 : (c + 1) * OWN]


def merge_kernel(parts, out):
    stat = parts[pl.ds(OWN, PEERS, stride=CHUNK), :]
    high = jnp.max(stat, axis=0, keepdims=True)
    weight = jnp.exp2(jnp.minimum(stat - high, 0.0))
    total = jnp.sum(pltpu.roll(weight, OWN, 1) * stat, axis=0, keepdims=True)
    rows = []
    for r in range(OWN):
        part = parts[pl.ds(r, PEERS, stride=CHUNK), :]
        got = jnp.sum(part * weight[:, r : r + 1], axis=0, keepdims=True)
        rows.append(got / total[:, OWN + r : OWN + r + 1])
    out[...] = jnp.concatenate(rows, axis=0).astype(BF16)


def call(kernel, outs, specs, scratch=(), out_specs=None, limit=VMEM_LIMIT):
    return pl.pallas_call(
        kernel,
        out_shape=outs,
        in_specs=specs,
        out_specs=out_specs or jax.tree.map(lambda _: VMEM, outs),
        scratch_shapes=scratch,
        compiler_params=pltpu.CompilerParams(vmem_limit_bytes=limit),
    )


def turn(value, axis, step):
    size = lax.axis_size(axis)
    return lax.ppermute(value, axis, [(i, (i + step) % size) for i in range(size)])


def local(
    queries,
    row_branch,
    suffix_len,
    common_keys,
    common_values,
    branch_keys,
    branch_values,
    suffix_keys,
    suffix_values,
):
    width = KV_HEADS * HEAD_DIM
    flat = [
        a.reshape(-1, width)
        for a in (common_keys, common_values, branch_keys, branch_values, suffix_keys, suffix_values)
    ]
    block = (2 * KEYS, HEAD_DIM)
    block = (2 * KEYS, HEAD_DIM)
    packed = call(
        pack_kernel,
        [jax.ShapeDtypeStruct((OWN_ROOM, HEAD_DIM), BF16)]
        + [jax.ShapeDtypeStruct(block, BF16)] * (N_X - 1),
        [HBM] * 8,
        [
            pltpu.VMEM((2 * KEYS, width), BF16),
            pltpu.VMEM((N_X, *block), BF16),
            pltpu.VMEM((INFO, HEAD_DIM), BF16),
            pltpu.SMEM((ROWS,), jnp.int32),
            pltpu.SMEM((OWN,), jnp.int32),
            pltpu.SMEM((2 * OWN,), jnp.int32),
            pltpu.SemaphoreType.DMA((8,)),
            pltpu.SemaphoreType.DMA((N_X, 7)),
        ],
        [HBM] * N_X,
        PACK_LIMIT,
    )(row_branch, suffix_len, *flat)
    kvs = {i: turn(packed[i], "x", i) for i in (1, 3, 2)}
    kvs = [kvs[i] for i in range(1, N_X)]

    q = jnp.broadcast_to(queries[None], (PEERS, OWN, HEAD_DIM))
    q = lax.all_to_all(q, PLANE, split_axis=0, concat_axis=0, tiled=True)
    q = q.reshape(LINES, HEAD_DIM)
    parts = call(
        attend_kernel,
        jax.ShapeDtypeStruct((PEERS * CHUNK, HEAD_DIM), F32),
        [HBM] + [VMEM] * 4,
        [pltpu.VMEM((2 * KEYS + INFO, HEAD_DIM), BF16), pltpu.SemaphoreType.DMA],
    )(packed[0], q, *kvs)
    parts = parts.reshape(PEERS * CHUNK, 1, HEAD_DIM)
    parts = lax.all_to_all(parts, PLANE, split_axis=0, concat_axis=0, tiled=True)
    parts = parts.reshape(PEERS * CHUNK, HEAD_DIM)
    return call(merge_kernel, jax.ShapeDtypeStruct((OWN, HEAD_DIM), BF16), [VMEM])(parts)


def solution(mesh):
    axes = ("ylo", "z", "x", "yhi", "core")
    fine = Mesh(mesh.devices.reshape(N_YLO, N_Z, N_X, N_YHI, N_CORE), axes)
    branch, seq = ("ylo", "z"), ("x", "yhi", "core")
    return jax.shard_map(
        local,
        mesh=fine,
        in_specs=(
            P(branch, seq),
            P(),
            P(branch),
            P(branch + seq, None),
            P(branch + seq, None),
            P(branch, seq, None),
            P(branch, seq, None),
            P(branch, seq, None),
            P(branch, seq, None),
        ),
        out_specs=P(branch, seq),
        check_vma=False,
    )
```

```python
import functools
import math

import jax
import jax.numpy as jnp
from jax import lax
from jax.experimental import pallas as pl
from jax.experimental.pallas import tpu as pltpu
from jax.sharding import Mesh
from jax.sharding import PartitionSpec as P

HEADS = 32
KV_HEADS = 4
GROUP = HEADS // KV_HEADS
HEAD_DIM = 128
N_X, N_YHI, N_CORE, N_YLO, N_Z = 4, 4, 2, 2, 8
PLANE = ("z", "yhi", "ylo", "core")
PEERS = N_Z * N_YHI * N_YLO * N_CORE
ROWS = 64
OWN = 4
COM, BRA, SUF = 256, 512, 64
KEYS = COM + BRA + OWN * SUF
LINES = PEERS * OWN
PICKED = OWN * GROUP
INFO = 16
OWN_ROOM = 1 << 16
CHUNK = OWN + 1
LOW = -1e30
F32 = jnp.float32
BF16 = jnp.bfloat16
SCALE = math.log2(math.e) / math.sqrt(HEAD_DIM)
VMEM = pl.BlockSpec(memory_space=pltpu.VMEM)
HBM = pl.BlockSpec(memory_space=pltpu.HBM)
VMEM_LIMIT = 48 * 1024 * 1024
PACK_LIMIT = 57 * 1024 * 1024


def pack_kernel(queries, row_branch, suffix_len, ck, cv, bk, bv, sk, sv, *rest):
    repeated, outs = rest[0], rest[1 : 1 + N_X]
    held, blocks, info, lines, line_room, branch_of, live, pick, sem, out_sem = rest[1 + N_X :]
    x = lax.axis_index("x")
    branch = lax.axis_index("ylo") * N_Z + lax.axis_index("z")
    small = [
        pltpu.make_async_copy(row_branch, branch_of, sem.at[6]),
        pltpu.make_async_copy(suffix_len, live, sem.at[7]),
        pltpu.make_async_copy(queries, lines, sem.at[8]),
    ]
    copies, at = [], 0
    for n, (src, count) in enumerate(
        ((ck, COM), (bk, BRA), (sk, OWN * SUF), (cv, COM), (bv, BRA), (sv, OWN * SUF))
    ):
        rows = pl.ds(at, count)
        copies.append((pltpu.make_async_copy(src, held.at[rows], sem.at[n]), rows))
        at += count
    for copy in (*small, *(copy for copy, _ in copies)):
        copy.start()
    for copy in small:
        copy.wait()
    found = jnp.int32(0)
    for i in range(ROWS):
        pick[found] = jnp.int32(i)
        found = found + (branch_of[i] == branch).astype(jnp.int32)
    row = lax.broadcasted_iota(jnp.int32, info.shape, 0)
    words = jnp.zeros(info.shape, jnp.int32)
    for j in range(OWN):
        words = jnp.where(row == j, pick[j], words)
        words = jnp.where(row == OWN + j, live[j] >> 4, words)
        words = jnp.where(row == 2 * OWN + j, live[j] & 15, words)
    info[...] = words.astype(F32).astype(BF16)
    line_room[...] = jnp.broadcast_to(lines[...], line_room.shape)
    sent = [
        pltpu.make_async_copy(info, outs[0].at[pl.ds(2 * KEYS, INFO)], out_sem.at[0, 6]),
        pltpu.make_async_copy(line_room, repeated, out_sem.at[1, 6]),
    ]
    for out in sent:
        out.start()
    for n, (copy, rows) in enumerate(copies):
        copy.wait()
        for i in (1, 3, 2, 0):
            head = lax.rem(x + i, N_X)
            cols = pl.ds(pl.multiple_of(head * HEAD_DIM, HEAD_DIM), HEAD_DIM)
            blocks[i, rows] = held[rows, cols]
            out = pltpu.make_async_copy(blocks.at[i, rows], outs[i].at[rows], out_sem.at[i, n])
            out.start()
            sent.append(out)
    for out in sent:
        out.wait()


def score(q, key, mask=None):
    s = lax.dot_general(q, key, (((1,), (1,)), ((), ())), preferred_element_type=F32) * SCALE
    return s if mask is None else jnp.where(mask, s, LOW)


def weigh(scores, values, masks=None):
    top = jnp.max(functools.reduce(jnp.maximum, scores), axis=1, keepdims=True)
    total = out = None
    for i, (s, value) in enumerate(zip(scores, values)):
        w = jnp.exp2(s - top)
        if masks is not None:
            w = jnp.where(masks[i], w, 0.0)
        o = jnp.dot(w.astype(BF16), value, preferred_element_type=F32)
        total = w if total is None else total + w
        out = o if out is None else out + o
    return out, top, jnp.sum(total, axis=1, keepdims=True)


def picked_lines(picks, axis):
    shape = (2 * PICKED, 1) if axis == 0 else (1, 2 * PICKED)
    branch = lax.axis_index("ylo") * N_Z + lax.axis_index("z")
    at = lax.broadcasted_iota(jnp.int32, shape, axis)
    row = branch * OWN + ((at >> 3) & (OWN - 1))
    for j in range(OWN):
        row = jnp.where(at >> 3 == j, jnp.broadcast_to(picks[j], shape), row)
    ylo, z, r = row >> 5, (row >> 2) & 7, row & 3
    yhi, core = (at >> 1) & 3, at & 1
    return (((z * N_YHI + yhi) * N_YLO + ylo) * N_CORE + core) * OWN + r


def attend_kernel(own_hbm, q_ref, kv1, kv2, kv3, out_ref, own, info, sem):
    x, yhi, core = (lax.axis_index(a) for a in ("x", "yhi", "core"))
    words_load = pltpu.make_async_copy(own_hbm.at[pl.ds(2 * KEYS, INFO)], info, sem.at[0])
    own_load = pltpu.make_async_copy(own_hbm.at[pl.ds(0, 2 * KEYS)], own, sem.at[1])
    words_load.start()
    own_load.start()
    kvs = [kv1, kv2, kv3, own]
    sources = [lax.rem(x + N_X - i, N_X) for i in (1, 2, 3, 0)]
    suffix = (COM + BRA, OWN * SUF)

    def key(kv, at, count):
        return kv[pl.ds(at, count)]

    def values(at, count):
        return [kv[pl.ds(KEYS + at, count)] for kv in kvs]

    q = q_ref[...]
    scores = [score(q, key(kv, 0, COM)) for kv in kvs[:-1]]

    words_load.wait()
    words = info[...].astype(F32).astype(jnp.int32)
    words = [words[j : j + 1, 0:1] for j in range(3 * OWN)]
    picks = words[:OWN]
    lives = [16 * words[OWN + j] + words[2 * OWN + j] for j in range(OWN)]
    shape = (2 * PICKED, LINES)
    select = lax.broadcasted_iota(jnp.int32, shape, 1) == picked_lines(picks, 0)
    q_sel = jnp.dot(select.astype(F32).astype(BF16), q, preferred_element_type=F32).astype(BF16)

    shape = (PICKED, OWN * SUF)
    q_row = lax.broadcasted_iota(jnp.int32, shape, 0) >> 3
    slot = lax.broadcasted_iota(jnp.int32, (1, OWN * SUF), 1)
    k_row, slot = slot >> 6, slot & (SUF - 1)
    live = jnp.zeros(k_row.shape, jnp.int32)
    for j in range(OWN):
        live = jnp.where(k_row == j, jnp.broadcast_to(lives[j], live.shape), live)
    masks = []
    for source in sources:
        first = ((source * N_YHI + yhi) * N_CORE + core) * SUF
        masks.append(q_row == jnp.where(slot + first < live, k_row, -1))

    b_scores = [score(q_sel[:PICKED], key(kv, COM, BRA)) for kv in kvs[:-1]]
    s_scores = [score(q_sel[PICKED:], key(kv, *suffix), mask) for kv, mask in zip(kvs[:-1], masks)]
    own_load.wait()
    scores.append(score(q, key(own, 0, COM)))
    b_scores.append(score(q_sel[:PICKED], key(own, COM, BRA)))
    s_scores.append(score(q_sel[PICKED:], key(own, *suffix), masks[-1]))
    out, top, total = weigh(scores, values(0, COM))
    b_out, b_top, b_total = weigh(b_scores, values(COM, BRA))
    s_out, s_top, s_total = weigh(s_scores, values(*suffix), masks)

    square = (2 * PICKED, 2 * PICKED)
    eye = lax.broadcasted_iota(jnp.int32, square, 0) == lax.broadcasted_iota(jnp.int32, square, 1)

    def across(a, b):
        col = jnp.broadcast_to(jnp.concatenate([a, b], axis=0), square)
        return jnp.sum(jnp.where(eye, col, 0.0), axis=0, keepdims=True)

    shape = (LINES, 2 * PICKED)
    place_of = lax.broadcasted_iota(jnp.int32, shape, 0) == picked_lines(picks, 1)
    p_top = jnp.where(place_of, jnp.broadcast_to(across(b_top, s_top), shape), LOW)
    high = jnp.maximum(top, jnp.max(p_top, axis=1, keepdims=True))
    weight = jnp.where(place_of, jnp.exp2(p_top - high), 0.0)
    scale = jnp.exp2(top - high)
    parts = jnp.concatenate([b_out, s_out], axis=0)
    out = out * scale + jnp.dot(
        weight, parts, precision=lax.Precision.HIGHEST, preferred_element_type=F32
    )
    total = total * scale + jnp.sum(weight * across(b_total, s_total), axis=1, keepdims=True)

    shape = (LINES, HEAD_DIM)
    lane = lax.broadcasted_iota(jnp.int32, shape, 1)
    r = lax.broadcasted_iota(jnp.int32, shape, 0) & (OWN - 1)
    stat = jnp.where(lane == r, high, 0.0) + jnp.where(lane == r + OWN, total, 0.0)
    stat = sum(pltpu.roll(stat, i, 0) for i in range(1, OWN)) + stat
    for c in range(PEERS):
        out_ref[pl.ds(c * CHUNK, OWN)] = out[c * OWN : (c + 1) * OWN]
        out_ref[pl.ds(c * CHUNK + OWN, 1)] = stat[(c + 1) * OWN - 1 : (c + 1) * OWN]


def merge_kernel(parts, out):
    stat = parts[pl.ds(OWN, PEERS, stride=CHUNK), :]
    high = jnp.max(stat, axis=0, keepdims=True)
    weight = jnp.exp2(jnp.minimum(stat - high, 0.0))
    total = jnp.sum(pltpu.roll(weight, OWN, 1) * stat, axis=0, keepdims=True)
    rows = []
    for r in range(OWN):
        part = parts[pl.ds(r, PEERS, stride=CHUNK), :]
        got = jnp.sum(part * weight[:, r : r + 1], axis=0, keepdims=True)
        rows.append(got / total[:, OWN + r : OWN + r + 1])
    out[...] = jnp.concatenate(rows, axis=0).astype(BF16)


def call(kernel, outs, specs, scratch=(), out_specs=None, limit=VMEM_LIMIT):
    return pl.pallas_call(
        kernel,
        out_shape=outs,
        in_specs=specs,
        out_specs=out_specs or jax.tree.map(lambda _: VMEM, outs),
        scratch_shapes=scratch,
        compiler_params=pltpu.CompilerParams(vmem_limit_bytes=limit),
    )


def turn(value, axis, step):
    size = lax.axis_size(axis)
    return lax.ppermute(value, axis, [(i, (i + step) % size) for i in range(size)])


def local(
    queries,
    row_branch,
    suffix_len,
    common_keys,
    common_values,
    branch_keys,
    branch_values,
    suffix_keys,
    suffix_values,
):
    width = KV_HEADS * HEAD_DIM
    flat = [
        a.reshape(-1, width)
        for a in (common_keys, common_values, branch_keys, branch_values, suffix_keys, suffix_values)
    ]
    block = (2 * KEYS, HEAD_DIM)
    block = (2 * KEYS, HEAD_DIM)
    q, *packed = call(
        pack_kernel,
        [
            jax.ShapeDtypeStruct((PEERS, OWN, HEAD_DIM), BF16),
            jax.ShapeDtypeStruct((OWN_ROOM, HEAD_DIM), BF16),
        ]
        + [jax.ShapeDtypeStruct(block, BF16)] * (N_X - 1),
        [HBM] * 9,
        [
            pltpu.VMEM((2 * KEYS, width), BF16),
            pltpu.VMEM((N_X, *block), BF16),
            pltpu.VMEM((INFO, HEAD_DIM), BF16),
            pltpu.VMEM((1, OWN, HEAD_DIM), BF16),
            pltpu.VMEM((PEERS, OWN, HEAD_DIM), BF16),
            pltpu.SMEM((ROWS,), jnp.int32),
            pltpu.SMEM((OWN,), jnp.int32),
            pltpu.SMEM((2 * OWN,), jnp.int32),
            pltpu.SemaphoreType.DMA((9,)),
            pltpu.SemaphoreType.DMA((N_X, 7)),
        ],
        [HBM] * (1 + N_X),
        PACK_LIMIT,
    )(queries[None], row_branch, suffix_len, *flat)
    kvs = {i: turn(packed[i], "x", i) for i in (1, 3, 2)}
    kvs = [kvs[i] for i in range(1, N_X)]

    q = lax.all_to_all(q, PLANE, split_axis=0, concat_axis=0, tiled=True)
    q = q.reshape(LINES, HEAD_DIM)
    parts = call(
        attend_kernel,
        jax.ShapeDtypeStruct((PEERS * CHUNK, HEAD_DIM), F32),
        [HBM] + [VMEM] * 4,
        [
            pltpu.VMEM(block, BF16),
            pltpu.VMEM((INFO, HEAD_DIM), BF16),
            pltpu.SemaphoreType.DMA((2,)),
        ],
    )(packed[0], q, *kvs)
    parts = parts.reshape(PEERS * CHUNK, 1, HEAD_DIM)
    parts = lax.all_to_all(parts, PLANE, split_axis=0, concat_axis=0, tiled=True)
    parts = parts.reshape(PEERS * CHUNK, HEAD_DIM)
    return call(merge_kernel, jax.ShapeDtypeStruct((OWN, HEAD_DIM), BF16), [VMEM])(parts)


def solution(mesh):
    axes = ("ylo", "z", "x", "yhi", "core")
    fine = Mesh(mesh.devices.reshape(N_YLO, N_Z, N_X, N_YHI, N_CORE), axes)
    branch, seq = ("ylo", "z"), ("x", "yhi", "core")
    return jax.shard_map(
        local,
        mesh=fine,
        in_specs=(
            P(branch, seq),
            P(),
            P(branch),
            P(branch + seq, None),
            P(branch + seq, None),
            P(branch, seq, None),
            P(branch, seq, None),
            P(branch, seq, None),
            P(branch, seq, None),
        ),
        out_specs=P(branch, seq),
        check_vma=False,
    )
```

```python
import functools
import math

import jax
import jax.numpy as jnp
from jax import lax
from jax.experimental import pallas as pl
from jax.experimental.pallas import tpu as pltpu
from jax.sharding import Mesh
from jax.sharding import PartitionSpec as P

HEADS = 32
KV_HEADS = 4
GROUP = HEADS // KV_HEADS
HEAD_DIM = 128
N_X, N_YHI, N_CORE, N_YLO, N_Z = 4, 4, 2, 2, 8
PLANE = ("z", "yhi", "ylo", "core")
PEERS = N_Z * N_YHI * N_YLO * N_CORE
STEPS = (2, 1, 3)
ROWS = 64
OWN = 4
COM, BRA, SUF = 256, 512, 64
KEYS = COM + BRA + OWN * SUF
LINES = PEERS * OWN
PICKED = OWN * GROUP
INFO = 16
OWN_ROOM = 1 << 16
CHUNK = OWN + 1
LOW = -1e30
F32 = jnp.float32
BF16 = jnp.bfloat16
SCALE = math.log2(math.e) / math.sqrt(HEAD_DIM)
VMEM = pl.BlockSpec(memory_space=pltpu.VMEM)
HBM = pl.BlockSpec(memory_space=pltpu.HBM)
VMEM_LIMIT = 48 * 1024 * 1024
PACK_LIMIT = 57 * 1024 * 1024


def pack_kernel(queries, row_branch, suffix_len, ck, cv, bk, bv, sk, sv, *rest):
    repeated, outs = rest[0], rest[1 : 1 + N_X]
    held, blocks, info, lines, line_room, branch_of, live, pick, sem, out_sem = rest[1 + N_X :]
    x = lax.axis_index("x")
    branch = lax.axis_index("ylo") * N_Z + lax.axis_index("z")
    small = [
        pltpu.make_async_copy(row_branch, branch_of, sem.at[6]),
        pltpu.make_async_copy(suffix_len, live, sem.at[7]),
        pltpu.make_async_copy(queries, lines, sem.at[8]),
    ]
    copies, at = [], 0
    for n, (src, count) in enumerate(
        ((ck, COM), (bk, BRA), (sk, OWN * SUF), (cv, COM), (bv, BRA), (sv, OWN * SUF))
    ):
        rows = pl.ds(at, count)
        copies.append((pltpu.make_async_copy(src, held.at[rows], sem.at[n]), rows))
        at += count
    for copy in (*small, *(copy for copy, _ in copies)):
        copy.start()
    for copy in small:
        copy.wait()
    found = jnp.int32(0)
    for i in range(ROWS):
        pick[found] = jnp.int32(i)
        found = found + (branch_of[i] == branch).astype(jnp.int32)
    row = lax.broadcasted_iota(jnp.int32, info.shape, 0)
    words = jnp.zeros(info.shape, jnp.int32)
    for j in range(OWN):
        words = jnp.where(row == j, pick[j], words)
        words = jnp.where(row == OWN + j, live[j] >> 4, words)
        words = jnp.where(row == 2 * OWN + j, live[j] & 15, words)
    info[...] = words.astype(F32).astype(BF16)
    line_room[...] = jnp.broadcast_to(lines[...], line_room.shape)
    sent = [
        pltpu.make_async_copy(info, outs[0].at[pl.ds(2 * KEYS, INFO)], out_sem.at[0, 6]),
        pltpu.make_async_copy(line_room, repeated, out_sem.at[1, 6]),
    ]
    for out in sent:
        out.start()
    for n, (copy, rows) in enumerate(copies):
        copy.wait()
        for i in (1, 3, 2, 0):
            head = lax.rem(x + i, N_X)
            cols = pl.ds(pl.multiple_of(head * HEAD_DIM, HEAD_DIM), HEAD_DIM)
            blocks[i, rows] = held[rows, cols]
            out = pltpu.make_async_copy(blocks.at[i, rows], outs[i].at[rows], out_sem.at[i, n])
            out.start()
            sent.append(out)
    for out in sent:
        out.wait()


def score(q, key, mask=None):
    s = lax.dot_general(q, key, (((1,), (1,)), ((), ())), preferred_element_type=F32) * SCALE
    return s if mask is None else jnp.where(mask, s, LOW)


def weigh(scores, values, masks=None):
    top = jnp.max(functools.reduce(jnp.maximum, scores), axis=1, keepdims=True)
    total = out = None
    for i, (s, value) in enumerate(zip(scores, values)):
        w = jnp.exp2(s - top)
        if masks is not None:
            w = jnp.where(masks[i], w, 0.0)
        o = jnp.dot(w.astype(BF16), value, preferred_element_type=F32)
        total = w if total is None else total + w
        out = o if out is None else out + o
    return out, top, jnp.sum(total, axis=1, keepdims=True)


def picked_lines(picks, axis):
    shape = (2 * PICKED, 1) if axis == 0 else (1, 4 * PICKED)
    branch = lax.axis_index("ylo") * N_Z + lax.axis_index("z")
    at = lax.broadcasted_iota(jnp.int32, shape, axis) & (2 * PICKED - 1)
    row = branch * OWN + ((at >> 3) & (OWN - 1))
    for j in range(OWN):
        row = jnp.where(at >> 3 == j, jnp.broadcast_to(picks[j], shape), row)
    ylo, z, r = row >> 5, (row >> 2) & 7, row & 3
    yhi, core = (at >> 1) & 3, at & 1
    return (((z * N_YHI + yhi) * N_YLO + ylo) * N_CORE + core) * OWN + r


def attend_kernel(own_hbm, q_ref, kv_a, kv_b, kv_c, out_ref, own, info, sem):
    x, yhi, core = (lax.axis_index(a) for a in ("x", "yhi", "core"))
    words_load = pltpu.make_async_copy(own_hbm.at[pl.ds(2 * KEYS, INFO)], info, sem.at[0])
    own_load = pltpu.make_async_copy(own_hbm.at[pl.ds(0, 2 * KEYS)], own, sem.at[1])
    words_load.start()
    own_load.start()
    kvs = [kv_a, kv_b, kv_c, own]
    sources = [lax.rem(x + N_X - i, N_X) for i in (*STEPS, 0)]
    suffix = (COM + BRA, OWN * SUF)

    def key(kv, at, count):
        return kv[pl.ds(at, count)]

    def values(at, count):
        return [kv[pl.ds(KEYS + at, count)] for kv in kvs]

    q = q_ref[...]
    scores = [score(q, key(kv, 0, COM)) for kv in kvs[:-1]]

    words_load.wait()
    words = info[...].astype(F32).astype(jnp.int32)
    words = [words[j : j + 1, 0:1] for j in range(3 * OWN)]
    picks = words[:OWN]
    lives = [16 * words[OWN + j] + words[2 * OWN + j] for j in range(OWN)]
    shape = (2 * PICKED, LINES)
    select = lax.broadcasted_iota(jnp.int32, shape, 1) == picked_lines(picks, 0)
    q_sel = jnp.dot(select.astype(F32).astype(BF16), q, preferred_element_type=F32).astype(BF16)

    shape = (PICKED, OWN * SUF)
    q_row = lax.broadcasted_iota(jnp.int32, shape, 0) >> 3
    slot = lax.broadcasted_iota(jnp.int32, (1, OWN * SUF), 1)
    k_row, slot = slot >> 6, slot & (SUF - 1)
    live = jnp.zeros(k_row.shape, jnp.int32)
    for j in range(OWN):
        live = jnp.where(k_row == j, jnp.broadcast_to(lives[j], live.shape), live)
    masks = []
    for source in sources:
        first = ((source * N_YHI + yhi) * N_CORE + core) * SUF
        masks.append(q_row == jnp.where(slot + first < live, k_row, -1))

    b_scores = [score(q_sel[:PICKED], key(kv, COM, BRA)) for kv in kvs[:-1]]
    s_scores = [score(q_sel[PICKED:], key(kv, *suffix), mask) for kv, mask in zip(kvs[:-1], masks)]
    own_load.wait()
    scores.append(score(q, key(own, 0, COM)))
    b_scores.append(score(q_sel[:PICKED], key(own, COM, BRA)))
    s_scores.append(score(q_sel[PICKED:], key(own, *suffix), masks[-1]))
    out, top, total = weigh(scores, values(0, COM))
    b_out, b_top, b_total = weigh(b_scores, values(COM, BRA))
    s_out, s_top, s_total = weigh(s_scores, values(*suffix), masks)

    square = (2 * PICKED, 4 * PICKED)
    column = lax.broadcasted_iota(jnp.int32, square, 1)
    eye = lax.broadcasted_iota(jnp.int32, square, 0) == column & (2 * PICKED - 1)

    def across(a, b):
        col = jnp.broadcast_to(jnp.concatenate([a, b], axis=0), square)
        return jnp.sum(jnp.where(eye, col, 0.0), axis=0, keepdims=True)

    shape = (LINES, 4 * PICKED)
    place_of = lax.broadcasted_iota(jnp.int32, shape, 0) == picked_lines(picks, 1)
    first = lax.broadcasted_iota(jnp.int32, shape, 1) < 2 * PICKED
    p_top = jnp.where(place_of, jnp.broadcast_to(across(b_top, s_top), shape), LOW)
    high = jnp.maximum(top, jnp.max(p_top, axis=1, keepdims=True))
    weight = jnp.where(place_of, jnp.exp2(p_top - high), 0.0)
    scale = jnp.exp2(top - high)
    near = weight.astype(BF16).astype(F32)
    weights = [jnp.where(first, near, weight - near), jnp.where(first, near, 0.0)]
    parts = jnp.concatenate([b_out, s_out], axis=0)
    p_near = parts.astype(BF16).astype(F32)
    parts = [p_near, p_near, parts - p_near, jnp.zeros_like(parts)]
    out = out * scale + jnp.dot(
        jnp.concatenate(weights, axis=1).astype(BF16),
        jnp.concatenate(parts, axis=0).astype(BF16),
        preferred_element_type=F32,
    )
    weight = jnp.where(first, weight, 0.0)
    total = total * scale + jnp.sum(weight * across(b_total, s_total), axis=1, keepdims=True)

    shape = (LINES, HEAD_DIM)
    lane = lax.broadcasted_iota(jnp.int32, shape, 1)
    r = lax.broadcasted_iota(jnp.int32, shape, 0) & (OWN - 1)
    stat = jnp.where(lane == r, high, 0.0) + jnp.where(lane == r + OWN, total, 0.0)
    stat = sum(pltpu.roll(stat, i, 0) for i in range(1, OWN)) + stat
    for c in range(PEERS):
        out_ref[pl.ds(c * CHUNK, OWN)] = out[c * OWN : (c + 1) * OWN]
        out_ref[pl.ds(c * CHUNK + OWN, 1)] = stat[(c + 1) * OWN - 1 : (c + 1) * OWN]


def merge_kernel(parts, out):
    stat = parts[pl.ds(OWN, PEERS, stride=CHUNK), :]
    high = jnp.max(stat, axis=0, keepdims=True)
    weight = jnp.exp2(jnp.minimum(stat - high, 0.0))
    total = jnp.sum(pltpu.roll(weight, OWN, 1) * stat, axis=0, keepdims=True)
    rows = []
    for r in range(OWN):
        part = parts[pl.ds(r, PEERS, stride=CHUNK), :]
        got = jnp.sum(part * weight[:, r : r + 1], axis=0, keepdims=True)
        rows.append(got / total[:, OWN + r : OWN + r + 1])
    out[...] = jnp.concatenate(rows, axis=0).astype(BF16)


def call(kernel, outs, specs, scratch=(), out_specs=None, limit=VMEM_LIMIT):
    return pl.pallas_call(
        kernel,
        out_shape=outs,
        in_specs=specs,
        out_specs=out_specs or jax.tree.map(lambda _: VMEM, outs),
        scratch_shapes=scratch,
        compiler_params=pltpu.CompilerParams(vmem_limit_bytes=limit),
    )


def turn(value, axis, step):
    size = lax.axis_size(axis)
    return lax.ppermute(value, axis, [(i, (i + step) % size) for i in range(size)])


def local(
    queries,
    row_branch,
    suffix_len,
    common_keys,
    common_values,
    branch_keys,
    branch_values,
    suffix_keys,
    suffix_values,
):
    width = KV_HEADS * HEAD_DIM
    flat = [
        a.reshape(-1, width)
        for a in (common_keys, common_values, branch_keys, branch_values, suffix_keys, suffix_values)
    ]
    block = (2 * KEYS, HEAD_DIM)
    block = (2 * KEYS, HEAD_DIM)
    q, *packed = call(
        pack_kernel,
        [
            jax.ShapeDtypeStruct((PEERS, OWN, HEAD_DIM), BF16),
            jax.ShapeDtypeStruct((OWN_ROOM, HEAD_DIM), BF16),
        ]
        + [jax.ShapeDtypeStruct(block, BF16)] * (N_X - 1),
        [HBM] * 9,
        [
            pltpu.VMEM((2 * KEYS, width), BF16),
            pltpu.VMEM((N_X, *block), BF16),
            pltpu.VMEM((INFO, HEAD_DIM), BF16),
            pltpu.VMEM((1, OWN, HEAD_DIM), BF16),
            pltpu.VMEM((PEERS, OWN, HEAD_DIM), BF16),
            pltpu.SMEM((ROWS,), jnp.int32),
            pltpu.SMEM((OWN,), jnp.int32),
            pltpu.SMEM((2 * OWN,), jnp.int32),
            pltpu.SemaphoreType.DMA((9,)),
            pltpu.SemaphoreType.DMA((N_X, 7)),
        ],
        [HBM] * (1 + N_X),
        PACK_LIMIT,
    )(queries[None], row_branch, suffix_len, *flat)
    kvs = [turn(packed[i], "x", i) for i in STEPS]

    q = lax.all_to_all(q, PLANE, split_axis=0, concat_axis=0, tiled=True)
    q = q.reshape(LINES, HEAD_DIM)
    parts = call(
        attend_kernel,
        jax.ShapeDtypeStruct((PEERS * CHUNK, HEAD_DIM), F32),
        [HBM] + [VMEM] * 4,
        [
            pltpu.VMEM(block, BF16),
            pltpu.VMEM((INFO, HEAD_DIM), BF16),
            pltpu.SemaphoreType.DMA((2,)),
        ],
    )(packed[0], q, *kvs)
    parts = parts.reshape(PEERS * CHUNK, 1, HEAD_DIM)
    parts = lax.all_to_all(parts, PLANE, split_axis=0, concat_axis=0, tiled=True)
    parts = parts.reshape(PEERS * CHUNK, HEAD_DIM)
    return call(merge_kernel, jax.ShapeDtypeStruct((OWN, HEAD_DIM), BF16), [VMEM])(parts)


def solution(mesh):
    axes = ("ylo", "z", "x", "yhi", "core")
    fine = Mesh(mesh.devices.reshape(N_YLO, N_Z, N_X, N_YHI, N_CORE), axes)
    branch, seq = ("ylo", "z"), ("x", "yhi", "core")
    return jax.shard_map(
        local,
        mesh=fine,
        in_specs=(
            P(branch, seq),
            P(),
            P(branch),
            P(branch + seq, None),
            P(branch + seq, None),
            P(branch, seq, None),
            P(branch, seq, None),
            P(branch, seq, None),
            P(branch, seq, None),
        ),
        out_specs=P(branch, seq),
        check_vma=False,
    )
```

```python
import functools
import math

import jax
import jax.numpy as jnp
from jax import lax
from jax.experimental import pallas as pl
from jax.experimental.pallas import tpu as pltpu
from jax.sharding import Mesh
from jax.sharding import PartitionSpec as P

HEADS = 32
KV_HEADS = 4
GROUP = HEADS // KV_HEADS
HEAD_DIM = 128
N_X, N_YHI, N_CORE, N_YLO, N_Z = 4, 4, 2, 2, 8
PLANE = ("z", "yhi", "ylo", "core")
PEERS = N_Z * N_YHI * N_YLO * N_CORE
STEPS = (2, 1, 3)
ROWS = 64
OWN = 4
COM, BRA, SUF = 256, 512, 64
KEYS = COM + BRA + OWN * SUF
LINES = PEERS * OWN
PICKED = OWN * GROUP
INFO = 16
OWN_ROOM = 1 << 16
CHUNK = OWN + 2
TOP_AT, TOTAL_AT, POWER_AT = (0, 4, 8), (16, 20, 24), 32
LOW = -1e30
F32 = jnp.float32
BF16 = jnp.bfloat16
SCALE = math.log2(math.e) / math.sqrt(HEAD_DIM)
VMEM = pl.BlockSpec(memory_space=pltpu.VMEM)
HBM = pl.BlockSpec(memory_space=pltpu.HBM)
VMEM_LIMIT = 48 * 1024 * 1024
PACK_LIMIT = 57 * 1024 * 1024


def pack_kernel(queries, row_branch, suffix_len, ck, cv, bk, bv, sk, sv, *rest):
    repeated, outs = rest[0], rest[1 : 1 + N_X]
    held, blocks, info, lines, line_room, branch_of, live, pick, sem, out_sem = rest[1 + N_X :]
    x = lax.axis_index("x")
    branch = lax.axis_index("ylo") * N_Z + lax.axis_index("z")
    small = [
        pltpu.make_async_copy(row_branch, branch_of, sem.at[6]),
        pltpu.make_async_copy(suffix_len, live, sem.at[7]),
        pltpu.make_async_copy(queries, lines, sem.at[8]),
    ]
    copies, at = [], 0
    for n, (src, count) in enumerate(
        ((ck, COM), (bk, BRA), (sk, OWN * SUF), (cv, COM), (bv, BRA), (sv, OWN * SUF))
    ):
        rows = pl.ds(at, count)
        copies.append((pltpu.make_async_copy(src, held.at[rows], sem.at[n]), rows))
        at += count
    for copy in (*small, *(copy for copy, _ in copies)):
        copy.start()
    for copy in small:
        copy.wait()
    found = jnp.int32(0)
    for i in range(ROWS):
        pick[found] = jnp.int32(i)
        found = found + (branch_of[i] == branch).astype(jnp.int32)
    row = lax.broadcasted_iota(jnp.int32, info.shape, 0)
    words = jnp.zeros(info.shape, jnp.int32)
    for j in range(OWN):
        words = jnp.where(row == j, pick[j], words)
        words = jnp.where(row == OWN + j, live[j] >> 4, words)
        words = jnp.where(row == 2 * OWN + j, live[j] & 15, words)
    info[...] = words.astype(F32).astype(BF16)
    line_room[...] = jnp.broadcast_to(lines[...], line_room.shape)
    sent = [
        pltpu.make_async_copy(info, outs[0].at[pl.ds(2 * KEYS, INFO)], out_sem.at[0, 6]),
        pltpu.make_async_copy(line_room, repeated, out_sem.at[1, 6]),
    ]
    for out in sent:
        out.start()
    for n, (copy, rows) in enumerate(copies):
        copy.wait()
        for i in (1, 3, 2, 0):
            head = lax.rem(x + i, N_X)
            cols = pl.ds(pl.multiple_of(head * HEAD_DIM, HEAD_DIM), HEAD_DIM)
            blocks[i, rows] = held[rows, cols]
            out = pltpu.make_async_copy(blocks.at[i, rows], outs[i].at[rows], out_sem.at[i, n])
            out.start()
            sent.append(out)
    for out in sent:
        out.wait()


def score(q, key, mask=None):
    s = lax.dot_general(q, key, (((1,), (1,)), ((), ())), preferred_element_type=F32) * SCALE
    return s if mask is None else jnp.where(mask, s, LOW)


def weigh(scores, values, masks=None):
    top = jnp.max(functools.reduce(jnp.maximum, scores), axis=1, keepdims=True)
    total = out = None
    for i, (s, value) in enumerate(zip(scores, values)):
        w = jnp.exp2(s - top)
        if masks is not None:
            w = jnp.where(masks[i], w, 0.0)
        o = jnp.dot(w.astype(BF16), value, preferred_element_type=F32)
        total = w if total is None else total + w
        out = o if out is None else out + o
    return out, top, jnp.sum(total, axis=1, keepdims=True)


def picked_lines(picks, axis):
    shape = (2 * PICKED, 1) if axis == 0 else (1, 4 * PICKED)
    branch = lax.axis_index("ylo") * N_Z + lax.axis_index("z")
    at = lax.broadcasted_iota(jnp.int32, shape, axis) & (2 * PICKED - 1)
    row = branch * OWN + ((at >> 3) & (OWN - 1))
    for j in range(OWN):
        row = jnp.where(at >> 3 == j, jnp.broadcast_to(picks[j], shape), row)
    ylo, z, r = row >> 5, (row >> 2) & 7, row & 3
    yhi, core = (at >> 1) & 3, at & 1
    return (((z * N_YHI + yhi) * N_YLO + ylo) * N_CORE + core) * OWN + r


def attend_kernel(own_hbm, q_ref, kv_a, kv_b, kv_c, out_ref, own, info, sem):
    x, yhi, core = (lax.axis_index(a) for a in ("x", "yhi", "core"))
    words_load = pltpu.make_async_copy(own_hbm.at[pl.ds(2 * KEYS, INFO)], info, sem.at[0])
    own_load = pltpu.make_async_copy(own_hbm.at[pl.ds(0, 2 * KEYS)], own, sem.at[1])
    words_load.start()
    own_load.start()
    kvs = [kv_a, kv_b, kv_c, own]
    sources = [lax.rem(x + N_X - i, N_X) for i in (*STEPS, 0)]
    suffix = (COM + BRA, OWN * SUF)

    def key(kv, at, count):
        return kv[pl.ds(at, count)]

    def values(at, count):
        return [kv[pl.ds(KEYS + at, count)] for kv in kvs]

    q = q_ref[...]
    scores = [score(q, key(kv, 0, COM)) for kv in kvs[:-1]]

    words_load.wait()
    words = info[...].astype(F32).astype(jnp.int32)
    words = [words[j : j + 1, 0:1] for j in range(3 * OWN)]
    picks = words[:OWN]
    lives = [16 * words[OWN + j] + words[2 * OWN + j] for j in range(OWN)]
    shape = (2 * PICKED, LINES)
    select = lax.broadcasted_iota(jnp.int32, shape, 1) == picked_lines(picks, 0)
    q_sel = jnp.dot(select.astype(F32).astype(BF16), q, preferred_element_type=F32).astype(BF16)

    shape = (PICKED, OWN * SUF)
    q_row = lax.broadcasted_iota(jnp.int32, shape, 0) >> 3
    slot = lax.broadcasted_iota(jnp.int32, (1, OWN * SUF), 1)
    k_row, slot = slot >> 6, slot & (SUF - 1)
    live = jnp.zeros(k_row.shape, jnp.int32)
    for j in range(OWN):
        live = jnp.where(k_row == j, jnp.broadcast_to(lives[j], live.shape), live)
    masks = []
    for source in sources:
        first = ((source * N_YHI + yhi) * N_CORE + core) * SUF
        masks.append(q_row == jnp.where(slot + first < live, k_row, -1))

    b_scores = [score(q_sel[:PICKED], key(kv, COM, BRA)) for kv in kvs[:-1]]
    s_scores = [score(q_sel[PICKED:], key(kv, *suffix), mask) for kv, mask in zip(kvs[:-1], masks)]
    own_load.wait()
    scores.append(score(q, key(own, 0, COM)))
    b_scores.append(score(q_sel[:PICKED], key(own, COM, BRA)))
    s_scores.append(score(q_sel[PICKED:], key(own, *suffix), masks[-1]))
    out, top, total = weigh(scores, values(0, COM))
    b_out, b_top, b_total = weigh(b_scores, values(COM, BRA))
    s_out, s_top, s_total = weigh(s_scores, values(*suffix), masks)

    square = (2 * PICKED, 4 * PICKED)
    column = lax.broadcasted_iota(jnp.int32, square, 1)
    eye = lax.broadcasted_iota(jnp.int32, square, 0) == column & (2 * PICKED - 1)

    def across(a, b):
        col = jnp.broadcast_to(jnp.concatenate([a, b], axis=0), square)
        return jnp.sum(jnp.where(eye, col, 0.0), axis=0, keepdims=True)

    shape = (LINES, 4 * PICKED)
    place_of = lax.broadcasted_iota(jnp.int32, shape, 0) == picked_lines(picks, 1)
    first = lax.broadcasted_iota(jnp.int32, shape, 1) < 2 * PICKED
    p_top = jnp.where(place_of, jnp.broadcast_to(across(b_top, s_top), shape), LOW)
    high = jnp.maximum(top, jnp.max(p_top, axis=1, keepdims=True))
    weight = jnp.where(place_of, jnp.exp2(p_top - high), 0.0)
    scale = jnp.exp2(top - high)
    near = weight.astype(BF16).astype(F32)
    weights = [jnp.where(first, near, weight - near), jnp.where(first, near, 0.0)]
    parts = jnp.concatenate([b_out, s_out], axis=0)
    p_near = parts.astype(BF16).astype(F32)
    parts = [p_near, p_near, parts - p_near, jnp.zeros_like(parts)]
    out = out * scale + jnp.dot(
        jnp.concatenate(weights, axis=1).astype(BF16),
        jnp.concatenate(parts, axis=0).astype(BF16),
        preferred_element_type=F32,
    )
    weight = jnp.where(first, weight, 0.0)
    total = total * scale + jnp.sum(weight * across(b_total, s_total), axis=1, keepdims=True)

    power = jnp.ceil(jnp.log(jnp.max(jnp.abs(out), axis=1, keepdims=True)) * math.log2(math.e))
    power = jnp.clip(power, -120.0, 120.0)
    out = out * jnp.exp2(-power)
    shape = (LINES, HEAD_DIM)
    r = lax.broadcasted_iota(jnp.int32, shape, 0) & (OWN - 1)
    lane = lax.broadcasted_iota(jnp.int32, shape, 1) - r
    stat = jnp.where(lane == POWER_AT, power, 0.0)
    for value, lanes in ((high, TOP_AT), (total, TOTAL_AT)):
        for at in lanes:
            piece = value.astype(BF16).astype(F32)
            stat = jnp.where(lane == at, piece, stat)
            value = value - piece
    stat = sum(pltpu.roll(stat, i, 0) for i in range(1, OWN)) + stat
    for c in range(PEERS):
        out_ref[pl.ds(c * CHUNK, OWN)] = out[c * OWN : (c + 1) * OWN]
        out_ref[pl.ds(c * CHUNK + OWN, 2)] = stat[(c + 1) * OWN - 2 : (c + 1) * OWN]


def merge_kernel(parts, out):
    stat = parts[pl.ds(CHUNK - 1, PEERS, stride=CHUNK), :]

    def value(*lanes):
        return sum(pltpu.roll(stat, (HEAD_DIM - at) % HEAD_DIM, 1) for at in lanes)

    top = value(*TOP_AT)
    high = jnp.max(top, axis=0, keepdims=True)
    weight = jnp.exp2(jnp.minimum(top - high, 0.0))
    total = jnp.sum(weight * value(*TOTAL_AT), axis=0, keepdims=True)
    weight = weight * jnp.exp2(value(POWER_AT))
    rows = []
    for r in range(OWN):
        part = parts[pl.ds(r, PEERS, stride=CHUNK), :]
        got = jnp.sum(part * weight[:, r : r + 1], axis=0, keepdims=True)
        rows.append(got / total[:, r : r + 1])
    out[...] = jnp.concatenate(rows, axis=0).astype(BF16)


def call(kernel, outs, specs, scratch=(), out_specs=None, limit=VMEM_LIMIT):
    return pl.pallas_call(
        kernel,
        out_shape=outs,
        in_specs=specs,
        out_specs=out_specs or jax.tree.map(lambda _: VMEM, outs),
        scratch_shapes=scratch,
        compiler_params=pltpu.CompilerParams(vmem_limit_bytes=limit),
    )


def turn(value, axis, step):
    size = lax.axis_size(axis)
    return lax.ppermute(value, axis, [(i, (i + step) % size) for i in range(size)])


def local(
    queries,
    row_branch,
    suffix_len,
    common_keys,
    common_values,
    branch_keys,
    branch_values,
    suffix_keys,
    suffix_values,
):
    width = KV_HEADS * HEAD_DIM
    flat = [
        a.reshape(-1, width)
        for a in (common_keys, common_values, branch_keys, branch_values, suffix_keys, suffix_values)
    ]
    block = (2 * KEYS, HEAD_DIM)
    block = (2 * KEYS, HEAD_DIM)
    q, *packed = call(
        pack_kernel,
        [
            jax.ShapeDtypeStruct((PEERS, OWN, HEAD_DIM), BF16),
            jax.ShapeDtypeStruct((OWN_ROOM, HEAD_DIM), BF16),
        ]
        + [jax.ShapeDtypeStruct(block, BF16)] * (N_X - 1),
        [HBM] * 9,
        [
            pltpu.VMEM((2 * KEYS, width), BF16),
            pltpu.VMEM((N_X, *block), BF16),
            pltpu.VMEM((INFO, HEAD_DIM), BF16),
            pltpu.VMEM((1, OWN, HEAD_DIM), BF16),
            pltpu.VMEM((PEERS, OWN, HEAD_DIM), BF16),
            pltpu.SMEM((ROWS,), jnp.int32),
            pltpu.SMEM((OWN,), jnp.int32),
            pltpu.SMEM((2 * OWN,), jnp.int32),
            pltpu.SemaphoreType.DMA((9,)),
            pltpu.SemaphoreType.DMA((N_X, 7)),
        ],
        [HBM] * (1 + N_X),
        PACK_LIMIT,
    )(queries[None], row_branch, suffix_len, *flat)
    kvs = [turn(packed[i], "x", i) for i in STEPS]

    q = lax.all_to_all(q, PLANE, split_axis=0, concat_axis=0, tiled=True)
    q = q.reshape(LINES, HEAD_DIM)
    parts = call(
        attend_kernel,
        jax.ShapeDtypeStruct((PEERS * CHUNK, HEAD_DIM), F32),
        [HBM] + [VMEM] * 4,
        [
            pltpu.VMEM(block, BF16),
            pltpu.VMEM((INFO, HEAD_DIM), BF16),
            pltpu.SemaphoreType.DMA((2,)),
        ],
    )(packed[0], q, *kvs)
    parts = parts.astype(jnp.float16).reshape(PEERS * CHUNK // 2, 2, HEAD_DIM)
    parts = lax.all_to_all(parts, PLANE, split_axis=0, concat_axis=0, tiled=True)
    parts = parts.reshape(PEERS * CHUNK, HEAD_DIM).astype(F32)
    return call(merge_kernel, jax.ShapeDtypeStruct((OWN, HEAD_DIM), BF16), [VMEM])(parts)


def solution(mesh):
    axes = ("ylo", "z", "x", "yhi", "core")
    fine = Mesh(mesh.devices.reshape(N_YLO, N_Z, N_X, N_YHI, N_CORE), axes)
    branch, seq = ("ylo", "z"), ("x", "yhi", "core")
    return jax.shard_map(
        local,
        mesh=fine,
        in_specs=(
            P(branch, seq),
            P(),
            P(branch),
            P(branch + seq, None),
            P(branch + seq, None),
            P(branch, seq, None),
            P(branch, seq, None),
            P(branch, seq, None),
            P(branch, seq, None),
        ),
        out_specs=P(branch, seq),
        check_vma=False,
    )
```

```python
import functools
import math

import jax
import jax.numpy as jnp
from jax import lax
from jax.experimental import pallas as pl
from jax.experimental.pallas import tpu as pltpu
from jax.sharding import Mesh
from jax.sharding import PartitionSpec as P

HEADS = 32
KV_HEADS = 4
GROUP = HEADS // KV_HEADS
HEAD_DIM = 128
N_X, N_YHI, N_CORE, N_YLO, N_Z = 4, 4, 2, 2, 8
PLANE = ("yhi", "ylo", "z", "core")
PEERS = N_Z * N_YHI * N_YLO * N_CORE
STEPS = (2, 3, 1)
ROWS = 64
OWN = 4
COM, BRA, SUF = 256, 512, 64
KEYS = COM + BRA + OWN * SUF
LINES = PEERS * OWN
PICKED = OWN * GROUP
INFO = 16
OWN_ROOM = 1 << 16
CHUNK = OWN + 2
TOP_AT, TOTAL_AT, POWER_AT = (0, 4, 8), (16, 20, 24), 32
LOW = -1e30
F32 = jnp.float32
BF16 = jnp.bfloat16
SCALE = math.log2(math.e) / math.sqrt(HEAD_DIM)
VMEM = pl.BlockSpec(memory_space=pltpu.VMEM)
HBM = pl.BlockSpec(memory_space=pltpu.HBM)
VMEM_LIMIT = 48 * 1024 * 1024
PACK_LIMIT = 57 * 1024 * 1024


def pack_kernel(queries, row_branch, suffix_len, ck, cv, bk, bv, sk, sv, *rest):
    repeated, outs = rest[0], rest[1 : 1 + N_X]
    held, blocks, info, lines, line_room, branch_of, live, pick, sem, out_sem = rest[1 + N_X :]
    x = lax.axis_index("x")
    branch = lax.axis_index("ylo") * N_Z + lax.axis_index("z")
    small = [
        pltpu.make_async_copy(row_branch, branch_of, sem.at[6]),
        pltpu.make_async_copy(suffix_len, live, sem.at[7]),
        pltpu.make_async_copy(queries, lines, sem.at[8]),
    ]
    copies, at = [], 0
    for n, (src, count) in enumerate(
        ((ck, COM), (bk, BRA), (sk, OWN * SUF), (cv, COM), (bv, BRA), (sv, OWN * SUF))
    ):
        rows = pl.ds(at, count)
        copies.append((pltpu.make_async_copy(src, held.at[rows], sem.at[n]), rows))
        at += count
    for copy in (*small, *(copy for copy, _ in copies)):
        copy.start()
    for copy in small:
        copy.wait()
    found = jnp.int32(0)
    for i in range(ROWS):
        pick[found] = jnp.int32(i)
        found = found + (branch_of[i] == branch).astype(jnp.int32)
    row = lax.broadcasted_iota(jnp.int32, info.shape, 0)
    words = jnp.zeros(info.shape, jnp.int32)
    for j in range(OWN):
        words = jnp.where(row == j, pick[j], words)
        words = jnp.where(row == OWN + j, live[j] >> 4, words)
        words = jnp.where(row == 2 * OWN + j, live[j] & 15, words)
    info[...] = words.astype(F32).astype(BF16)
    line_room[...] = jnp.broadcast_to(lines[...], line_room.shape)
    sent = [
        pltpu.make_async_copy(info, outs[0].at[pl.ds(2 * KEYS, INFO)], out_sem.at[0, 6]),
        pltpu.make_async_copy(line_room, repeated, out_sem.at[1, 6]),
    ]
    for out in sent:
        out.start()
    for n, (copy, rows) in enumerate(copies):
        copy.wait()
        for i in (1, 3, 2, 0):
            head = lax.rem(x + i, N_X)
            cols = pl.ds(pl.multiple_of(head * HEAD_DIM, HEAD_DIM), HEAD_DIM)
            blocks[i, rows] = held[rows, cols]
            out = pltpu.make_async_copy(blocks.at[i, rows], outs[i].at[rows], out_sem.at[i, n])
            out.start()
            sent.append(out)
    for out in sent:
        out.wait()


def score(q, key, mask=None):
    s = lax.dot_general(q, key, (((1,), (1,)), ((), ())), preferred_element_type=F32) * SCALE
    return s if mask is None else jnp.where(mask, s, LOW)


def weigh(scores, values, masks=None):
    top = jnp.max(functools.reduce(jnp.maximum, scores), axis=1, keepdims=True)
    total = out = None
    for i, (s, value) in enumerate(zip(scores, values)):
        w = jnp.exp2(s - top)
        if masks is not None:
            w = jnp.where(masks[i], w, 0.0)
        o = jnp.dot(w.astype(BF16), value, preferred_element_type=F32)
        total = w if total is None else total + w
        out = o if out is None else out + o
    return out, top, jnp.sum(total, axis=1, keepdims=True)


def picked_lines(picks, axis):
    shape = (2 * PICKED, 1) if axis == 0 else (1, 4 * PICKED)
    branch = lax.axis_index("ylo") * N_Z + lax.axis_index("z")
    at = lax.broadcasted_iota(jnp.int32, shape, axis) & (2 * PICKED - 1)
    row = branch * OWN + ((at >> 3) & (OWN - 1))
    for j in range(OWN):
        row = jnp.where(at >> 3 == j, jnp.broadcast_to(picks[j], shape), row)
    place = {"ylo": row >> 5, "z": (row >> 2) & 7, "yhi": (at >> 1) & 3, "core": at & 1}
    size = {"ylo": N_YLO, "z": N_Z, "yhi": N_YHI, "core": N_CORE}
    line = 0
    for axis_name in PLANE:
        line = line * size[axis_name] + place[axis_name]
    return line * OWN + (row & 3)


def attend_kernel(own_hbm, q_ref, kv_a, kv_b, kv_c, out_ref, own, info, sem):
    x, yhi, core = (lax.axis_index(a) for a in ("x", "yhi", "core"))
    words_load = pltpu.make_async_copy(own_hbm.at[pl.ds(2 * KEYS, INFO)], info, sem.at[0])
    own_load = pltpu.make_async_copy(own_hbm.at[pl.ds(0, 2 * KEYS)], own, sem.at[1])
    words_load.start()
    own_load.start()
    kvs = [kv_a, kv_b, kv_c, own]
    sources = [lax.rem(x + N_X - i, N_X) for i in (*STEPS, 0)]
    suffix = (COM + BRA, OWN * SUF)

    def key(kv, at, count):
        return kv[pl.ds(at, count)]

    def values(at, count):
        return [kv[pl.ds(KEYS + at, count)] for kv in kvs]

    q = q_ref[...]
    scores = [score(q, key(kv, 0, COM)) for kv in kvs[:-1]]

    words_load.wait()
    words = info[...].astype(F32).astype(jnp.int32)
    words = [words[j : j + 1, 0:1] for j in range(3 * OWN)]
    picks = words[:OWN]
    lives = [16 * words[OWN + j] + words[2 * OWN + j] for j in range(OWN)]
    shape = (2 * PICKED, LINES)
    select = lax.broadcasted_iota(jnp.int32, shape, 1) == picked_lines(picks, 0)
    q_sel = jnp.dot(select.astype(F32).astype(BF16), q, preferred_element_type=F32).astype(BF16)

    shape = (PICKED, OWN * SUF)
    q_row = lax.broadcasted_iota(jnp.int32, shape, 0) >> 3
    slot = lax.broadcasted_iota(jnp.int32, (1, OWN * SUF), 1)
    k_row, slot = slot >> 6, slot & (SUF - 1)
    live = jnp.zeros(k_row.shape, jnp.int32)
    for j in range(OWN):
        live = jnp.where(k_row == j, jnp.broadcast_to(lives[j], live.shape), live)
    masks = []
    for source in sources:
        first = ((source * N_YHI + yhi) * N_CORE + core) * SUF
        masks.append(q_row == jnp.where(slot + first < live, k_row, -1))

    b_scores = [score(q_sel[:PICKED], key(kv, COM, BRA)) for kv in kvs[:-1]]
    s_scores = [score(q_sel[PICKED:], key(kv, *suffix), mask) for kv, mask in zip(kvs[:-1], masks)]
    own_load.wait()
    scores.append(score(q, key(own, 0, COM)))
    b_scores.append(score(q_sel[:PICKED], key(own, COM, BRA)))
    s_scores.append(score(q_sel[PICKED:], key(own, *suffix), masks[-1]))
    out, top, total = weigh(scores, values(0, COM))
    b_out, b_top, b_total = weigh(b_scores, values(COM, BRA))
    s_out, s_top, s_total = weigh(s_scores, values(*suffix), masks)

    square = (2 * PICKED, 4 * PICKED)
    column = lax.broadcasted_iota(jnp.int32, square, 1)
    eye = lax.broadcasted_iota(jnp.int32, square, 0) == column & (2 * PICKED - 1)

    def across(a, b):
        col = jnp.broadcast_to(jnp.concatenate([a, b], axis=0), square)
        return jnp.sum(jnp.where(eye, col, 0.0), axis=0, keepdims=True)

    shape = (LINES, 4 * PICKED)
    place_of = lax.broadcasted_iota(jnp.int32, shape, 0) == picked_lines(picks, 1)
    first = lax.broadcasted_iota(jnp.int32, shape, 1) < 2 * PICKED
    p_top = jnp.where(place_of, jnp.broadcast_to(across(b_top, s_top), shape), LOW)
    high = jnp.maximum(top, jnp.max(p_top, axis=1, keepdims=True))
    weight = jnp.where(place_of, jnp.exp2(p_top - high), 0.0)
    scale = jnp.exp2(top - high)
    near = weight.astype(BF16).astype(F32)
    weights = [jnp.where(first, near, weight - near), jnp.where(first, near, 0.0)]
    parts = jnp.concatenate([b_out, s_out], axis=0)
    p_near = parts.astype(BF16).astype(F32)
    parts = [p_near, p_near, parts - p_near, jnp.zeros_like(parts)]
    out = out * scale + jnp.dot(
        jnp.concatenate(weights, axis=1).astype(BF16),
        jnp.concatenate(parts, axis=0).astype(BF16),
        preferred_element_type=F32,
    )
    weight = jnp.where(first, weight, 0.0)
    total = total * scale + jnp.sum(weight * across(b_total, s_total), axis=1, keepdims=True)

    power = jnp.ceil(jnp.log(jnp.max(jnp.abs(out), axis=1, keepdims=True)) * math.log2(math.e))
    power = jnp.clip(power, -120.0, 120.0)
    out = out * jnp.exp2(-power)
    shape = (LINES, HEAD_DIM)
    r = lax.broadcasted_iota(jnp.int32, shape, 0) & (OWN - 1)
    lane = lax.broadcasted_iota(jnp.int32, shape, 1) - r
    stat = jnp.where(lane == POWER_AT, power, 0.0)
    for value, lanes in ((high, TOP_AT), (total, TOTAL_AT)):
        for at in lanes:
            piece = value.astype(BF16).astype(F32)
            stat = jnp.where(lane == at, piece, stat)
            value = value - piece
    stat = sum(pltpu.roll(stat, i, 0) for i in range(1, OWN)) + stat
    for c in range(PEERS):
        out_ref[pl.ds(c * CHUNK, OWN)] = out[c * OWN : (c + 1) * OWN]
        out_ref[pl.ds(c * CHUNK + OWN, 2)] = stat[(c + 1) * OWN - 2 : (c + 1) * OWN]


def merge_kernel(parts, out):
    stat = parts[pl.ds(CHUNK - 1, PEERS, stride=CHUNK), :]

    def value(*lanes):
        return sum(pltpu.roll(stat, (HEAD_DIM - at) % HEAD_DIM, 1) for at in lanes)

    top = value(*TOP_AT)
    high = jnp.max(top, axis=0, keepdims=True)
    weight = jnp.exp2(jnp.minimum(top - high, 0.0))
    total = jnp.sum(weight * value(*TOTAL_AT), axis=0, keepdims=True)
    weight = weight * jnp.exp2(value(POWER_AT))
    rows = []
    for r in range(OWN):
        part = parts[pl.ds(r, PEERS, stride=CHUNK), :]
        got = jnp.sum(part * weight[:, r : r + 1], axis=0, keepdims=True)
        rows.append(got / total[:, r : r + 1])
    out[...] = jnp.concatenate(rows, axis=0).astype(BF16)


def call(kernel, outs, specs, scratch=(), out_specs=None, limit=VMEM_LIMIT):
    return pl.pallas_call(
        kernel,
        out_shape=outs,
        in_specs=specs,
        out_specs=out_specs or jax.tree.map(lambda _: VMEM, outs),
        scratch_shapes=scratch,
        compiler_params=pltpu.CompilerParams(vmem_limit_bytes=limit),
    )


def turn(value, axis, step):
    size = lax.axis_size(axis)
    return lax.ppermute(value, axis, [(i, (i + step) % size) for i in range(size)])


def local(
    queries,
    row_branch,
    suffix_len,
    common_keys,
    common_values,
    branch_keys,
    branch_values,
    suffix_keys,
    suffix_values,
):
    width = KV_HEADS * HEAD_DIM
    flat = [
        a.reshape(-1, width)
        for a in (common_keys, common_values, branch_keys, branch_values, suffix_keys, suffix_values)
    ]
    block = (2 * KEYS, HEAD_DIM)
    block = (2 * KEYS, HEAD_DIM)
    q, *packed = call(
        pack_kernel,
        [
            jax.ShapeDtypeStruct((PEERS, OWN, HEAD_DIM), BF16),
            jax.ShapeDtypeStruct((OWN_ROOM, HEAD_DIM), BF16),
        ]
        + [jax.ShapeDtypeStruct(block, BF16)] * (N_X - 1),
        [HBM] * 9,
        [
            pltpu.VMEM((2 * KEYS, width), BF16),
            pltpu.VMEM((N_X, *block), BF16),
            pltpu.VMEM((INFO, HEAD_DIM), BF16),
            pltpu.VMEM((1, OWN, HEAD_DIM), BF16),
            pltpu.VMEM((PEERS, OWN, HEAD_DIM), BF16),
            pltpu.SMEM((ROWS,), jnp.int32),
            pltpu.SMEM((OWN,), jnp.int32),
            pltpu.SMEM((2 * OWN,), jnp.int32),
            pltpu.SemaphoreType.DMA((9,)),
            pltpu.SemaphoreType.DMA((N_X, 7)),
        ],
        [HBM] * (1 + N_X),
        PACK_LIMIT,
    )(queries[None], row_branch, suffix_len, *flat)
    kvs = [turn(packed[i], "x", i) for i in STEPS]

    q = lax.all_to_all(q, PLANE, split_axis=0, concat_axis=0, tiled=True)
    q = q.reshape(LINES, HEAD_DIM)
    parts = call(
        attend_kernel,
        jax.ShapeDtypeStruct((PEERS * CHUNK, HEAD_DIM), F32),
        [HBM] + [VMEM] * 4,
        [
            pltpu.VMEM(block, BF16),
            pltpu.VMEM((INFO, HEAD_DIM), BF16),
            pltpu.SemaphoreType.DMA((2,)),
        ],
    )(packed[0], q, *kvs)
    parts = parts.astype(jnp.float16).reshape(PEERS * CHUNK // 2, 2, HEAD_DIM)
    parts = lax.all_to_all(parts, PLANE, split_axis=0, concat_axis=0, tiled=True)
    parts = parts.reshape(PEERS * CHUNK, HEAD_DIM).astype(F32)
    return call(merge_kernel, jax.ShapeDtypeStruct((OWN, HEAD_DIM), BF16), [VMEM])(parts)


def solution(mesh):
    axes = ("ylo", "z", "x", "yhi", "core")
    fine = Mesh(mesh.devices.reshape(N_YLO, N_Z, N_X, N_YHI, N_CORE), axes)
    branch, seq = ("ylo", "z"), ("x", "yhi", "core")
    return jax.shard_map(
        local,
        mesh=fine,
        in_specs=(
            P(branch, seq),
            P(),
            P(branch),
            P(branch + seq, None),
            P(branch + seq, None),
            P(branch, seq, None),
            P(branch, seq, None),
            P(branch, seq, None),
            P(branch, seq, None),
        ),
        out_specs=P(branch, seq),
        check_vma=False,
    )
```

```python
import functools
import math

import jax
import jax.numpy as jnp
from jax import lax
from jax.experimental import pallas as pl
from jax.experimental.pallas import tpu as pltpu
from jax.sharding import Mesh
from jax.sharding import PartitionSpec as P

HEADS = 32
KV_HEADS = 4
GROUP = HEADS // KV_HEADS
HEAD_DIM = 128
N_X, N_YHI, N_CORE, N_YLO, N_Z = 4, 4, 2, 2, 8
PLANE = ("yhi", "ylo", "z", "core")
PEERS = N_Z * N_YHI * N_YLO * N_CORE
STEPS = (2, 3, 1)
ROWS = 64
OWN = 4
COM, BRA, SUF = 256, 512, 64
KEYS = COM + BRA + OWN * SUF
LINES = PEERS * OWN
PICKED = OWN * GROUP
INFO = 16
OWN_ROOM = 1 << 16
CHUNK = OWN + 2
TOP_AT, TOTAL_AT, POWER_AT = (0, 4, 8), (16, 20, 24), 32
LOW = -1e30
F32 = jnp.float32
BF16 = jnp.bfloat16
SCALE = math.log2(math.e) / math.sqrt(HEAD_DIM)
VMEM = pl.BlockSpec(memory_space=pltpu.VMEM)
HBM = pl.BlockSpec(memory_space=pltpu.HBM)
VMEM_LIMIT = 48 * 1024 * 1024
PACK_LIMIT = 57 * 1024 * 1024


def pack_kernel(queries, row_branch, suffix_len, ck, cv, bk, bv, sk, sv, *rest):
    repeated, outs = rest[0], rest[1 : 1 + N_X]
    held, blocks, info, lines, line_room, branch_of, live, pick, sem, out_sem = rest[1 + N_X :]
    x = lax.axis_index("x")
    branch = lax.axis_index("ylo") * N_Z + lax.axis_index("z")
    small = [
        pltpu.make_async_copy(row_branch, branch_of, sem.at[6]),
        pltpu.make_async_copy(suffix_len, live, sem.at[7]),
        pltpu.make_async_copy(queries, lines, sem.at[8]),
    ]
    copies, at = [], 0
    for n, (src, count) in enumerate(
        ((ck, COM), (bk, BRA), (sk, OWN * SUF), (cv, COM), (bv, BRA), (sv, OWN * SUF))
    ):
        rows = pl.ds(at, count)
        copies.append((pltpu.make_async_copy(src, held.at[rows], sem.at[n]), rows))
        at += count
    for copy in (*small, *(copy for copy, _ in copies)):
        copy.start()
    for copy in small:
        copy.wait()
    found = jnp.int32(0)
    for i in range(ROWS):
        pick[found] = jnp.int32(i)
        found = found + (branch_of[i] == branch).astype(jnp.int32)
    row = lax.broadcasted_iota(jnp.int32, info.shape, 0)
    words = jnp.zeros(info.shape, jnp.int32)
    for j in range(OWN):
        words = jnp.where(row == j, pick[j], words)
        words = jnp.where(row == OWN + j, live[j] >> 4, words)
        words = jnp.where(row == 2 * OWN + j, live[j] & 15, words)
    info[...] = words.astype(F32).astype(BF16)
    line_room[...] = jnp.broadcast_to(lines[...], line_room.shape)
    sent = [
        pltpu.make_async_copy(info, outs[0].at[pl.ds(2 * KEYS, INFO)], out_sem.at[0, 6]),
        pltpu.make_async_copy(line_room, repeated, out_sem.at[1, 6]),
    ]
    for out in sent:
        out.start()
    for n, (copy, rows) in enumerate(copies):
        copy.wait()
        for i in (1, 3, 2, 0):
            head = lax.rem(x + i, N_X)
            cols = pl.ds(pl.multiple_of(head * HEAD_DIM, HEAD_DIM), HEAD_DIM)
            blocks[i, rows] = held[rows, cols]
            out = pltpu.make_async_copy(blocks.at[i, rows], outs[i].at[rows], out_sem.at[i, n])
            out.start()
            sent.append(out)
    for out in sent:
        out.wait()


def score(q, key, mask=None):
    s = lax.dot_general(q, key, (((1,), (1,)), ((), ())), preferred_element_type=F32)
    return s if mask is None else jnp.where(mask, s, LOW)


def weigh(scores, values, masks=None):
    top = jnp.max(functools.reduce(jnp.maximum, scores), axis=1, keepdims=True)
    total = out = None
    for i, (s, value) in enumerate(zip(scores, values)):
        w = jnp.exp2((s - top) * SCALE)
        if masks is not None:
            w = jnp.where(masks[i], w, 0.0)
        o = jnp.dot(w.astype(BF16), value, preferred_element_type=F32)
        total = w if total is None else total + w
        out = o if out is None else out + o
    return out, top * SCALE, jnp.sum(total, axis=1, keepdims=True)


def picked_lines(picks, axis):
    shape = (2 * PICKED, 1) if axis == 0 else (1, 4 * PICKED)
    branch = lax.axis_index("ylo") * N_Z + lax.axis_index("z")
    at = lax.broadcasted_iota(jnp.int32, shape, axis) & (2 * PICKED - 1)
    row = branch * OWN + ((at >> 3) & (OWN - 1))
    for j in range(OWN):
        row = jnp.where(at >> 3 == j, jnp.broadcast_to(picks[j], shape), row)
    place = {"ylo": row >> 5, "z": (row >> 2) & 7, "yhi": (at >> 1) & 3, "core": at & 1}
    size = {"ylo": N_YLO, "z": N_Z, "yhi": N_YHI, "core": N_CORE}
    line = 0
    for axis_name in PLANE:
        line = line * size[axis_name] + place[axis_name]
    return line * OWN + (row & 3)


def attend_kernel(own_hbm, q_ref, kv_a, kv_b, kv_c, out_ref, own, info, sem):
    x, yhi, core = (lax.axis_index(a) for a in ("x", "yhi", "core"))
    words_load = pltpu.make_async_copy(own_hbm.at[pl.ds(2 * KEYS, INFO)], info, sem.at[0])
    own_load = pltpu.make_async_copy(own_hbm.at[pl.ds(0, 2 * KEYS)], own, sem.at[1])
    words_load.start()
    own_load.start()
    kvs = [kv_a, kv_b, kv_c, own]
    sources = [lax.rem(x + N_X - i, N_X) for i in (*STEPS, 0)]
    suffix = (COM + BRA, OWN * SUF)

    def key(kv, at, count):
        return kv[pl.ds(at, count)]

    def values(at, count):
        return [kv[pl.ds(KEYS + at, count)] for kv in kvs]

    q = q_ref[...]
    scores = [score(q, key(kv, 0, COM)) for kv in kvs[:-1]]

    words_load.wait()
    words = info[...].astype(F32).astype(jnp.int32)
    words = [words[j : j + 1, 0:1] for j in range(3 * OWN)]
    picks = words[:OWN]
    lives = [16 * words[OWN + j] + words[2 * OWN + j] for j in range(OWN)]
    shape = (2 * PICKED, LINES)
    select = lax.broadcasted_iota(jnp.int32, shape, 1) == picked_lines(picks, 0)
    q_sel = jnp.dot(select.astype(F32).astype(BF16), q, preferred_element_type=F32).astype(BF16)

    shape = (PICKED, OWN * SUF)
    q_row = lax.broadcasted_iota(jnp.int32, shape, 0) >> 3
    slot = lax.broadcasted_iota(jnp.int32, (1, OWN * SUF), 1)
    k_row, slot = slot >> 6, slot & (SUF - 1)
    live = jnp.zeros(k_row.shape, jnp.int32)
    for j in range(OWN):
        live = jnp.where(k_row == j, jnp.broadcast_to(lives[j], live.shape), live)
    masks = []
    for source in sources:
        first = ((source * N_YHI + yhi) * N_CORE + core) * SUF
        masks.append(q_row == jnp.where(slot + first < live, k_row, -1))

    b_scores = [score(q_sel[:PICKED], key(kv, COM, BRA)) for kv in kvs[:-1]]
    s_scores = [score(q_sel[PICKED:], key(kv, *suffix), mask) for kv, mask in zip(kvs[:-1], masks)]
    own_load.wait()
    scores.append(score(q, key(own, 0, COM)))
    b_scores.append(score(q_sel[:PICKED], key(own, COM, BRA)))
    s_scores.append(score(q_sel[PICKED:], key(own, *suffix), masks[-1]))
    out, top, total = weigh(scores, values(0, COM))
    b_out, b_top, b_total = weigh(b_scores, values(COM, BRA))
    s_out, s_top, s_total = weigh(s_scores, values(*suffix), masks)

    square = (2 * PICKED, 4 * PICKED)
    column = lax.broadcasted_iota(jnp.int32, square, 1)
    eye = lax.broadcasted_iota(jnp.int32, square, 0) == column & (2 * PICKED - 1)

    def across(a, b):
        col = jnp.broadcast_to(jnp.concatenate([a, b], axis=0), square)
        return jnp.sum(jnp.where(eye, col, 0.0), axis=0, keepdims=True)

    shape = (LINES, 4 * PICKED)
    place_of = lax.broadcasted_iota(jnp.int32, shape, 0) == picked_lines(picks, 1)
    first = lax.broadcasted_iota(jnp.int32, shape, 1) < 2 * PICKED
    p_top = jnp.where(place_of, jnp.broadcast_to(across(b_top, s_top), shape), LOW)
    high = jnp.maximum(top, jnp.max(p_top, axis=1, keepdims=True))
    weight = jnp.where(place_of, jnp.exp2(p_top - high), 0.0)
    scale = jnp.exp2(top - high)
    near = weight.astype(BF16).astype(F32)
    weights = [jnp.where(first, near, weight - near), jnp.where(first, near, 0.0)]
    parts = jnp.concatenate([b_out, s_out], axis=0)
    p_near = parts.astype(BF16).astype(F32)
    parts = [p_near, p_near, parts - p_near, jnp.zeros_like(parts)]
    out = out * scale + jnp.dot(
        jnp.concatenate(weights, axis=1).astype(BF16),
        jnp.concatenate(parts, axis=0).astype(BF16),
        preferred_element_type=F32,
    )
    weight = jnp.where(first, weight, 0.0)
    total = total * scale + jnp.sum(weight * across(b_total, s_total), axis=1, keepdims=True)

    power = jnp.ceil(jnp.log(jnp.max(jnp.abs(out), axis=1, keepdims=True)) * math.log2(math.e))
    power = jnp.clip(power, -120.0, 120.0)
    out = out * jnp.exp2(-power)
    shape = (LINES, HEAD_DIM)
    r = lax.broadcasted_iota(jnp.int32, shape, 0) & (OWN - 1)
    lane = lax.broadcasted_iota(jnp.int32, shape, 1) - r
    stat = jnp.where(lane == POWER_AT, power, 0.0)
    for value, lanes in ((high, TOP_AT), (total, TOTAL_AT)):
        for at in lanes:
            piece = value.astype(BF16).astype(F32)
            stat = jnp.where(lane == at, piece, stat)
            value = value - piece
    stat = sum(pltpu.roll(stat, i, 0) for i in range(1, OWN)) + stat
    for c in range(PEERS):
        out_ref[pl.ds(c * CHUNK, OWN)] = out[c * OWN : (c + 1) * OWN]
        out_ref[pl.ds(c * CHUNK + OWN, 2)] = stat[(c + 1) * OWN - 2 : (c + 1) * OWN]


def merge_kernel(parts, out):
    stat = parts[pl.ds(CHUNK - 1, PEERS, stride=CHUNK), :]

    def value(*lanes):
        return sum(pltpu.roll(stat, (HEAD_DIM - at) % HEAD_DIM, 1) for at in lanes)

    top = value(*TOP_AT)
    high = jnp.max(top, axis=0, keepdims=True)
    weight = jnp.exp2(jnp.minimum(top - high, 0.0))
    total = jnp.sum(weight * value(*TOTAL_AT), axis=0, keepdims=True)
    weight = weight * jnp.exp2(value(POWER_AT))
    rows = []
    for r in range(OWN):
        part = parts[pl.ds(r, PEERS, stride=CHUNK), :]
        got = jnp.sum(part * weight[:, r : r + 1], axis=0, keepdims=True)
        rows.append(got / total[:, r : r + 1])
    out[...] = jnp.concatenate(rows, axis=0).astype(BF16)


def call(kernel, outs, specs, scratch=(), out_specs=None, limit=VMEM_LIMIT):
    return pl.pallas_call(
        kernel,
        out_shape=outs,
        in_specs=specs,
        out_specs=out_specs or jax.tree.map(lambda _: VMEM, outs),
        scratch_shapes=scratch,
        compiler_params=pltpu.CompilerParams(vmem_limit_bytes=limit),
    )


def turn(value, axis, step):
    size = lax.axis_size(axis)
    return lax.ppermute(value, axis, [(i, (i + step) % size) for i in range(size)])


def local(
    queries,
    row_branch,
    suffix_len,
    common_keys,
    common_values,
    branch_keys,
    branch_values,
    suffix_keys,
    suffix_values,
):
    width = KV_HEADS * HEAD_DIM
    flat = [
        a.reshape(-1, width)
        for a in (common_keys, common_values, branch_keys, branch_values, suffix_keys, suffix_values)
    ]
    block = (2 * KEYS, HEAD_DIM)
    block = (2 * KEYS, HEAD_DIM)
    q, *packed = call(
        pack_kernel,
        [
            jax.ShapeDtypeStruct((PEERS, OWN, HEAD_DIM), BF16),
            jax.ShapeDtypeStruct((OWN_ROOM, HEAD_DIM), BF16),
        ]
        + [jax.ShapeDtypeStruct(block, BF16)] * (N_X - 1),
        [HBM] * 9,
        [
            pltpu.VMEM((2 * KEYS, width), BF16),
            pltpu.VMEM((N_X, *block), BF16),
            pltpu.VMEM((INFO, HEAD_DIM), BF16),
            pltpu.VMEM((1, OWN, HEAD_DIM), BF16),
            pltpu.VMEM((PEERS, OWN, HEAD_DIM), BF16),
            pltpu.SMEM((ROWS,), jnp.int32),
            pltpu.SMEM((OWN,), jnp.int32),
            pltpu.SMEM((2 * OWN,), jnp.int32),
            pltpu.SemaphoreType.DMA((9,)),
            pltpu.SemaphoreType.DMA((N_X, 7)),
        ],
        [HBM] * (1 + N_X),
        PACK_LIMIT,
    )(queries[None], row_branch, suffix_len, *flat)
    kvs = [turn(packed[i], "x", i) for i in STEPS]

    q = lax.all_to_all(q, PLANE, split_axis=0, concat_axis=0, tiled=True)
    q = q.reshape(LINES, HEAD_DIM)
    parts = call(
        attend_kernel,
        jax.ShapeDtypeStruct((PEERS * CHUNK, HEAD_DIM), F32),
        [HBM] + [VMEM] * 4,
        [
            pltpu.VMEM(block, BF16),
            pltpu.VMEM((INFO, HEAD_DIM), BF16),
            pltpu.SemaphoreType.DMA((2,)),
        ],
    )(packed[0], q, *kvs)
    parts = parts.astype(jnp.float16).reshape(PEERS * CHUNK // 2, 2, HEAD_DIM)
    parts = lax.all_to_all(parts, PLANE, split_axis=0, concat_axis=0, tiled=True)
    parts = parts.reshape(PEERS * CHUNK, HEAD_DIM).astype(F32)
    return call(merge_kernel, jax.ShapeDtypeStruct((OWN, HEAD_DIM), BF16), [VMEM])(parts)


def solution(mesh):
    axes = ("ylo", "z", "x", "yhi", "core")
    fine = Mesh(mesh.devices.reshape(N_YLO, N_Z, N_X, N_YHI, N_CORE), axes)
    branch, seq = ("ylo", "z"), ("x", "yhi", "core")
    return jax.shard_map(
        local,
        mesh=fine,
        in_specs=(
            P(branch, seq),
            P(),
            P(branch),
            P(branch + seq, None),
            P(branch + seq, None),
            P(branch, seq, None),
            P(branch, seq, None),
            P(branch, seq, None),
            P(branch, seq, None),
        ),
        out_specs=P(branch, seq),
        check_vma=False,
    )
```

```python
import functools
import math

import jax
import jax.numpy as jnp
from jax import lax
from jax.experimental import pallas as pl
from jax.experimental.pallas import tpu as pltpu
from jax.sharding import Mesh
from jax.sharding import PartitionSpec as P

HEADS = 32
KV_HEADS = 4
GROUP = HEADS // KV_HEADS
HEAD_DIM = 128
N_X, N_YHI, N_CORE, N_YLO, N_Z = 4, 4, 2, 2, 8
PLANE = ("yhi", "ylo", "z", "core")
PEERS = N_Z * N_YHI * N_YLO * N_CORE
STEPS = (2, 3, 1)
ROWS = 64
OWN = 4
COM, BRA, SUF = 256, 512, 64
KEYS = COM + BRA + OWN * SUF
LINES = PEERS * OWN
PICKED = OWN * GROUP
INFO = 16
OWN_ROOM = 1 << 16
CHUNK = OWN + 2
TOP_AT, TOTAL_AT, POWER_AT = (0, 4, 8), (16, 20), 32
LOW = -1e30
F32 = jnp.float32
BF16 = jnp.bfloat16
SCALE = math.log2(math.e) / math.sqrt(HEAD_DIM)
VMEM = pl.BlockSpec(memory_space=pltpu.VMEM)
HBM = pl.BlockSpec(memory_space=pltpu.HBM)
VMEM_LIMIT = 48 * 1024 * 1024
PACK_LIMIT = 57 * 1024 * 1024


def pack_kernel(queries, row_branch, suffix_len, ck, cv, bk, bv, sk, sv, *rest):
    repeated, outs = rest[0], rest[1 : 1 + N_X]
    held, blocks, info, lines, line_room, branch_of, live, pick, sem, out_sem = rest[1 + N_X :]
    x = lax.axis_index("x")
    branch = lax.axis_index("ylo") * N_Z + lax.axis_index("z")
    small = [
        pltpu.make_async_copy(row_branch, branch_of, sem.at[6]),
        pltpu.make_async_copy(suffix_len, live, sem.at[7]),
        pltpu.make_async_copy(queries, lines, sem.at[8]),
    ]
    copies, at = [], 0
    for n, (src, count) in enumerate(
        ((ck, COM), (bk, BRA), (sk, OWN * SUF), (cv, COM), (bv, BRA), (sv, OWN * SUF))
    ):
        rows = pl.ds(at, count)
        copies.append((pltpu.make_async_copy(src, held.at[rows], sem.at[n]), rows))
        at += count
    for copy in (*small, *(copy for copy, _ in copies)):
        copy.start()
    for copy in small:
        copy.wait()
    found = jnp.int32(0)
    for i in range(ROWS):
        pick[found] = jnp.int32(i)
        found = found + (branch_of[i] == branch).astype(jnp.int32)
    row = lax.broadcasted_iota(jnp.int32, info.shape, 0)
    words = jnp.zeros(info.shape, jnp.int32)
    for j in range(OWN):
        words = jnp.where(row == j, pick[j], words)
        words = jnp.where(row == OWN + j, live[j] >> 4, words)
        words = jnp.where(row == 2 * OWN + j, live[j] & 15, words)
    info[...] = words.astype(F32).astype(BF16)
    line_room[...] = jnp.broadcast_to(lines[...], line_room.shape)
    sent = [
        pltpu.make_async_copy(info, outs[0].at[pl.ds(2 * KEYS, INFO)], out_sem.at[0, 6]),
        pltpu.make_async_copy(line_room, repeated, out_sem.at[1, 6]),
    ]
    for out in sent:
        out.start()
    for n, (copy, rows) in enumerate(copies):
        copy.wait()
        for i in (1, 3, 2, 0):
            head = lax.rem(x + i, N_X)
            cols = pl.ds(pl.multiple_of(head * HEAD_DIM, HEAD_DIM), HEAD_DIM)
            blocks[i, rows] = held[rows, cols]
            out = pltpu.make_async_copy(blocks.at[i, rows], outs[i].at[rows], out_sem.at[i, n])
            out.start()
            sent.append(out)
    for out in sent:
        out.wait()


def score(q, key, mask=None):
    s = lax.dot_general(q, key, (((1,), (1,)), ((), ())), preferred_element_type=F32)
    return s if mask is None else jnp.where(mask, s, LOW)


def weigh(scores, values, masks=None):
    top = jnp.max(functools.reduce(jnp.maximum, scores), axis=1, keepdims=True)
    total = out = None
    for i, (s, value) in enumerate(zip(scores, values)):
        w = jnp.exp2((s - top) * SCALE)
        if masks is not None:
            w = jnp.where(masks[i], w, 0.0)
        o = jnp.dot(w.astype(BF16), value, preferred_element_type=F32)
        total = w if total is None else total + w
        out = o if out is None else out + o
    return out, top * SCALE, jnp.sum(total, axis=1, keepdims=True)


def picked_lines(picks, axis):
    shape = (2 * PICKED, 1) if axis == 0 else (1, 4 * PICKED)
    branch = lax.axis_index("ylo") * N_Z + lax.axis_index("z")
    at = lax.broadcasted_iota(jnp.int32, shape, axis) & (2 * PICKED - 1)
    row = branch * OWN + ((at >> 3) & (OWN - 1))
    for j in range(OWN):
        row = jnp.where(at >> 3 == j, jnp.broadcast_to(picks[j], shape), row)
    place = {"ylo": row >> 5, "z": (row >> 2) & 7, "yhi": (at >> 1) & 3, "core": at & 1}
    size = {"ylo": N_YLO, "z": N_Z, "yhi": N_YHI, "core": N_CORE}
    line = 0
    for axis_name in PLANE:
        line = line * size[axis_name] + place[axis_name]
    return line * OWN + (row & 3)


def attend_kernel(own_hbm, q_ref, kv_a, kv_b, kv_c, out_ref, own, info, sem):
    x, yhi, core = (lax.axis_index(a) for a in ("x", "yhi", "core"))
    words_load = pltpu.make_async_copy(own_hbm.at[pl.ds(2 * KEYS, INFO)], info, sem.at[0])
    own_load = pltpu.make_async_copy(own_hbm.at[pl.ds(0, 2 * KEYS)], own, sem.at[1])
    words_load.start()
    own_load.start()
    kvs = [kv_a, kv_b, kv_c, own]
    sources = [lax.rem(x + N_X - i, N_X) for i in (*STEPS, 0)]
    suffix = (COM + BRA, OWN * SUF)

    def key(kv, at, count):
        return kv[pl.ds(at, count)]

    def values(at, count):
        return [kv[pl.ds(KEYS + at, count)] for kv in kvs]

    q = q_ref[...]
    scores = [score(q, key(kv, 0, COM)) for kv in kvs[:-1]]

    words_load.wait()
    words = info[...].astype(F32).astype(jnp.int32)
    words = [words[j : j + 1, 0:1] for j in range(3 * OWN)]
    picks = words[:OWN]
    lives = [16 * words[OWN + j] + words[2 * OWN + j] for j in range(OWN)]
    shape = (2 * PICKED, LINES)
    select = lax.broadcasted_iota(jnp.int32, shape, 1) == picked_lines(picks, 0)
    q_sel = jnp.dot(select.astype(F32).astype(BF16), q, preferred_element_type=F32).astype(BF16)

    shape = (PICKED, OWN * SUF)
    q_row = lax.broadcasted_iota(jnp.int32, shape, 0) >> 3
    slot = lax.broadcasted_iota(jnp.int32, (1, OWN * SUF), 1)
    k_row, slot = slot >> 6, slot & (SUF - 1)
    live = jnp.zeros(k_row.shape, jnp.int32)
    for j in range(OWN):
        live = jnp.where(k_row == j, jnp.broadcast_to(lives[j], live.shape), live)
    masks = []
    for source in sources:
        first = ((source * N_YHI + yhi) * N_CORE + core) * SUF
        masks.append(q_row == jnp.where(slot + first < live, k_row, -1))

    b_scores = [score(q_sel[:PICKED], key(kv, COM, BRA)) for kv in kvs[:-1]]
    s_scores = [score(q_sel[PICKED:], key(kv, *suffix), mask) for kv, mask in zip(kvs[:-1], masks)]
    own_load.wait()
    scores.append(score(q, key(own, 0, COM)))
    b_scores.append(score(q_sel[:PICKED], key(own, COM, BRA)))
    s_scores.append(score(q_sel[PICKED:], key(own, *suffix), masks[-1]))
    out, top, total = weigh(scores, values(0, COM))
    b_out, b_top, b_total = weigh(b_scores, values(COM, BRA))
    s_out, s_top, s_total = weigh(s_scores, values(*suffix), masks)

    square = (2 * PICKED, 4 * PICKED)
    column = lax.broadcasted_iota(jnp.int32, square, 1)
    eye = lax.broadcasted_iota(jnp.int32, square, 0) == column & (2 * PICKED - 1)

    def across(a, b):
        col = jnp.broadcast_to(jnp.concatenate([a, b], axis=0), square)
        return jnp.sum(jnp.where(eye, col, 0.0), axis=0, keepdims=True)

    shape = (LINES, 4 * PICKED)
    place_of = lax.broadcasted_iota(jnp.int32, shape, 0) == picked_lines(picks, 1)
    first = lax.broadcasted_iota(jnp.int32, shape, 1) < 2 * PICKED
    p_top = jnp.where(place_of, jnp.broadcast_to(across(b_top, s_top), shape), LOW)
    high = jnp.maximum(top, jnp.max(p_top, axis=1, keepdims=True))
    weight = jnp.where(place_of, jnp.exp2(p_top - high), 0.0)
    scale = jnp.exp2(top - high)
    near = weight.astype(BF16).astype(F32)
    weights = [jnp.where(first, near, weight - near), jnp.where(first, near, 0.0)]
    parts = jnp.concatenate([b_out, s_out], axis=0)
    p_near = parts.astype(BF16).astype(F32)
    parts = [p_near, p_near, parts - p_near, jnp.zeros_like(parts)]
    out = out * scale + jnp.dot(
        jnp.concatenate(weights, axis=1).astype(BF16),
        jnp.concatenate(parts, axis=0).astype(BF16),
        preferred_element_type=F32,
    )
    weight = jnp.where(first, weight, 0.0)
    total = total * scale + jnp.sum(weight * across(b_total, s_total), axis=1, keepdims=True)

    power = jnp.ceil(jnp.log(jnp.max(jnp.abs(out), axis=1, keepdims=True)) * math.log2(math.e))
    power = jnp.clip(power, -120.0, 120.0)
    out = out * jnp.exp2(-power)
    shape = (LINES, HEAD_DIM)
    r = lax.broadcasted_iota(jnp.int32, shape, 0) & (OWN - 1)
    lane = lax.broadcasted_iota(jnp.int32, shape, 1) - r
    stat = jnp.where(lane == POWER_AT, power, 0.0)
    for value, lanes in ((high, TOP_AT), (total, TOTAL_AT)):
        for at in lanes:
            piece = value.astype(BF16).astype(F32)
            stat = jnp.where(lane == at, piece, stat)
            value = value - piece
    stat = stat + pltpu.roll(stat, 1, 0)
    stat = stat + pltpu.roll(stat, 2, 0)
    for c in range(PEERS):
        out_ref[pl.ds(c * CHUNK, OWN)] = out[c * OWN : (c + 1) * OWN]
        out_ref[pl.ds(c * CHUNK + OWN, 2)] = stat[(c + 1) * OWN - 2 : (c + 1) * OWN]


def merge_kernel(parts, out):
    stat = parts[pl.ds(CHUNK - 1, PEERS, stride=CHUNK), :]

    def value(*lanes):
        return sum(pltpu.roll(stat, (HEAD_DIM - at) % HEAD_DIM, 1) for at in lanes)

    top = value(*TOP_AT)
    high = jnp.max(top, axis=0, keepdims=True)
    weight = jnp.exp2(jnp.minimum(top - high, 0.0))
    total = jnp.sum(weight * value(*TOTAL_AT), axis=0, keepdims=True)
    weight = weight * jnp.exp2(value(POWER_AT))
    rows = []
    for r in range(OWN):
        part = parts[pl.ds(r, PEERS, stride=CHUNK), :]
        got = jnp.sum(part * weight[:, r : r + 1], axis=0, keepdims=True)
        rows.append(got / total[:, r : r + 1])
    out[...] = jnp.concatenate(rows, axis=0).astype(BF16)


def call(kernel, outs, specs, scratch=(), out_specs=None, limit=VMEM_LIMIT):
    return pl.pallas_call(
        kernel,
        out_shape=outs,
        in_specs=specs,
        out_specs=out_specs or jax.tree.map(lambda _: VMEM, outs),
        scratch_shapes=scratch,
        compiler_params=pltpu.CompilerParams(vmem_limit_bytes=limit),
    )


def turn(value, axis, step):
    size = lax.axis_size(axis)
    return lax.ppermute(value, axis, [(i, (i + step) % size) for i in range(size)])


def local(
    queries,
    row_branch,
    suffix_len,
    common_keys,
    common_values,
    branch_keys,
    branch_values,
    suffix_keys,
    suffix_values,
):
    width = KV_HEADS * HEAD_DIM
    flat = [
        a.reshape(-1, width)
        for a in (common_keys, common_values, branch_keys, branch_values, suffix_keys, suffix_values)
    ]
    block = (2 * KEYS, HEAD_DIM)
    block = (2 * KEYS, HEAD_DIM)
    q, *packed = call(
        pack_kernel,
        [
            jax.ShapeDtypeStruct((PEERS, OWN, HEAD_DIM), BF16),
            jax.ShapeDtypeStruct((OWN_ROOM, HEAD_DIM), BF16),
        ]
        + [jax.ShapeDtypeStruct(block, BF16)] * (N_X - 1),
        [HBM] * 9,
        [
            pltpu.VMEM((2 * KEYS, width), BF16),
            pltpu.VMEM((N_X, *block), BF16),
            pltpu.VMEM((INFO, HEAD_DIM), BF16),
            pltpu.VMEM((1, OWN, HEAD_DIM), BF16),
            pltpu.VMEM((PEERS, OWN, HEAD_DIM), BF16),
            pltpu.SMEM((ROWS,), jnp.int32),
            pltpu.SMEM((OWN,), jnp.int32),
            pltpu.SMEM((2 * OWN,), jnp.int32),
            pltpu.SemaphoreType.DMA((9,)),
            pltpu.SemaphoreType.DMA((N_X, 7)),
        ],
        [HBM] * (1 + N_X),
        PACK_LIMIT,
    )(queries[None], row_branch, suffix_len, *flat)
    kvs = [turn(packed[i], "x", i) for i in STEPS]

    q = lax.all_to_all(q, PLANE, split_axis=0, concat_axis=0, tiled=True)
    q = q.reshape(LINES, HEAD_DIM)
    parts = call(
        attend_kernel,
        jax.ShapeDtypeStruct((PEERS * CHUNK, HEAD_DIM), F32),
        [HBM] + [VMEM] * 4,
        [
            pltpu.VMEM(block, BF16),
            pltpu.VMEM((INFO, HEAD_DIM), BF16),
            pltpu.SemaphoreType.DMA((2,)),
        ],
    )(packed[0], q, *kvs)
    parts = parts.astype(jnp.float16).reshape(PEERS * CHUNK // 2, 2, HEAD_DIM)
    parts = lax.all_to_all(parts, PLANE, split_axis=0, concat_axis=0, tiled=True)
    parts = parts.reshape(PEERS * CHUNK, HEAD_DIM).astype(F32)
    return call(merge_kernel, jax.ShapeDtypeStruct((OWN, HEAD_DIM), BF16), [VMEM])(parts)


def solution(mesh):
    axes = ("ylo", "z", "x", "yhi", "core")
    fine = Mesh(mesh.devices.reshape(N_YLO, N_Z, N_X, N_YHI, N_CORE), axes)
    branch, seq = ("ylo", "z"), ("x", "yhi", "core")
    return jax.shard_map(
        local,
        mesh=fine,
        in_specs=(
            P(branch, seq),
            P(),
            P(branch),
            P(branch + seq, None),
            P(branch + seq, None),
            P(branch, seq, None),
            P(branch, seq, None),
            P(branch, seq, None),
            P(branch, seq, None),
        ),
        out_specs=P(branch, seq),
        check_vma=False,
    )
```

```python
import functools
import math

import jax
import jax.numpy as jnp
from jax import lax
from jax.experimental import pallas as pl
from jax.experimental.pallas import tpu as pltpu
from jax.sharding import Mesh
from jax.sharding import PartitionSpec as P

HEADS = 32
KV_HEADS = 4
GROUP = HEADS // KV_HEADS
HEAD_DIM = 128
N_X, N_YHI, N_CORE, N_YLO, N_Z = 4, 4, 2, 2, 8
PLANE = ("ylo", "yhi", "z", "core")
PEERS = N_Z * N_YHI * N_YLO * N_CORE
STEPS = (2, 3, 1)
ROWS = 64
OWN = 4
COM, BRA, SUF = 256, 512, 64
KEYS = COM + BRA + OWN * SUF
LINES = PEERS * OWN
PICKED = OWN * GROUP
INFO = 16
OWN_ROOM = 1 << 16
CHUNK = OWN + 2
TOP_AT, TOTAL_AT, POWER_AT = (0, 4, 8), (16, 20), 32
LOW = -1e30
F32 = jnp.float32
BF16 = jnp.bfloat16
SCALE = math.log2(math.e) / math.sqrt(HEAD_DIM)
VMEM = pl.BlockSpec(memory_space=pltpu.VMEM)
HBM = pl.BlockSpec(memory_space=pltpu.HBM)
VMEM_LIMIT = 48 * 1024 * 1024
PACK_LIMIT = 57 * 1024 * 1024


def pack_kernel(queries, row_branch, suffix_len, ck, cv, bk, bv, sk, sv, *rest):
    repeated, outs = rest[0], rest[1 : 1 + N_X]
    held, blocks, info, lines, line_room, branch_of, live, pick, sem, out_sem = rest[1 + N_X :]
    x = lax.axis_index("x")
    branch = lax.axis_index("ylo") * N_Z + lax.axis_index("z")
    small = [
        pltpu.make_async_copy(row_branch, branch_of, sem.at[6]),
        pltpu.make_async_copy(suffix_len, live, sem.at[7]),
        pltpu.make_async_copy(queries, lines, sem.at[8]),
    ]
    copies, at = [], 0
    for n, (src, count) in enumerate(
        ((ck, COM), (bk, BRA), (sk, OWN * SUF), (cv, COM), (bv, BRA), (sv, OWN * SUF))
    ):
        rows = pl.ds(at, count)
        copies.append((pltpu.make_async_copy(src, held.at[rows], sem.at[n]), rows))
        at += count
    for copy in (*small, *(copy for copy, _ in copies)):
        copy.start()
    for copy in small:
        copy.wait()
    found = jnp.int32(0)
    for i in range(ROWS):
        pick[found] = jnp.int32(i)
        found = found + (branch_of[i] == branch).astype(jnp.int32)
    row = lax.broadcasted_iota(jnp.int32, info.shape, 0)
    words = jnp.zeros(info.shape, jnp.int32)
    for j in range(OWN):
        words = jnp.where(row == j, pick[j], words)
        words = jnp.where(row == OWN + j, live[j] >> 4, words)
        words = jnp.where(row == 2 * OWN + j, live[j] & 15, words)
    info[...] = words.astype(F32).astype(BF16)
    line_room[...] = jnp.broadcast_to(lines[...], line_room.shape)
    sent = [
        pltpu.make_async_copy(info, outs[0].at[pl.ds(2 * KEYS, INFO)], out_sem.at[0, 6]),
        pltpu.make_async_copy(line_room, repeated, out_sem.at[1, 6]),
    ]
    for out in sent:
        out.start()
    for n, (copy, rows) in enumerate(copies):
        copy.wait()
        for i in (1, 3, 2, 0):
            head = lax.rem(x + i, N_X)
            cols = pl.ds(pl.multiple_of(head * HEAD_DIM, HEAD_DIM), HEAD_DIM)
            blocks[i, rows] = held[rows, cols]
            out = pltpu.make_async_copy(blocks.at[i, rows], outs[i].at[rows], out_sem.at[i, n])
            out.start()
            sent.append(out)
    for out in sent:
        out.wait()


def score(q, key, mask=None):
    s = lax.dot_general(q, key, (((1,), (1,)), ((), ())), preferred_element_type=F32)
    return s if mask is None else jnp.where(mask, s, LOW)


def weigh(scores, values, masks=None):
    top = jnp.max(functools.reduce(jnp.maximum, scores), axis=1, keepdims=True)
    total = out = None
    for i, (s, value) in enumerate(zip(scores, values)):
        w = jnp.exp2((s - top) * SCALE)
        if masks is not None:
            w = jnp.where(masks[i], w, 0.0)
        o = jnp.dot(w.astype(BF16), value, preferred_element_type=F32)
        total = w if total is None else total + w
        out = o if out is None else out + o
    return out, top * SCALE, jnp.sum(total, axis=1, keepdims=True)


def picked_lines(picks, axis):
    shape = (2 * PICKED, 1) if axis == 0 else (1, 4 * PICKED)
    branch = lax.axis_index("ylo") * N_Z + lax.axis_index("z")
    at = lax.broadcasted_iota(jnp.int32, shape, axis) & (2 * PICKED - 1)
    row = branch * OWN + ((at >> 3) & (OWN - 1))
    for j in range(OWN):
        row = jnp.where(at >> 3 == j, jnp.broadcast_to(picks[j], shape), row)
    place = {"ylo": row >> 5, "z": (row >> 2) & 7, "yhi": (at >> 1) & 3, "core": at & 1}
    size = {"ylo": N_YLO, "z": N_Z, "yhi": N_YHI, "core": N_CORE}
    line = 0
    for axis_name in PLANE:
        line = line * size[axis_name] + place[axis_name]
    return line * OWN + (row & 3)


def attend_kernel(own_hbm, q_ref, kv_a, kv_b, kv_c, out_ref, own, info, sem):
    x, yhi, core = (lax.axis_index(a) for a in ("x", "yhi", "core"))
    words_load = pltpu.make_async_copy(own_hbm.at[pl.ds(2 * KEYS, INFO)], info, sem.at[0])
    own_load = pltpu.make_async_copy(own_hbm.at[pl.ds(0, 2 * KEYS)], own, sem.at[1])
    words_load.start()
    own_load.start()
    kvs = [kv_a, kv_b, kv_c, own]
    sources = [lax.rem(x + N_X - i, N_X) for i in (*STEPS, 0)]
    suffix = (COM + BRA, OWN * SUF)

    def key(kv, at, count):
        return kv[pl.ds(at, count)]

    def values(at, count):
        return [kv[pl.ds(KEYS + at, count)] for kv in kvs]

    q = q_ref[...]
    scores = [score(q, key(kv, 0, COM)) for kv in kvs[:-1]]

    words_load.wait()
    words = info[...].astype(F32).astype(jnp.int32)
    words = [words[j : j + 1, 0:1] for j in range(3 * OWN)]
    picks = words[:OWN]
    lives = [16 * words[OWN + j] + words[2 * OWN + j] for j in range(OWN)]
    shape = (2 * PICKED, LINES)
    select = lax.broadcasted_iota(jnp.int32, shape, 1) == picked_lines(picks, 0)
    q_sel = jnp.dot(select.astype(F32).astype(BF16), q, preferred_element_type=F32).astype(BF16)

    shape = (PICKED, OWN * SUF)
    q_row = lax.broadcasted_iota(jnp.int32, shape, 0) >> 3
    slot = lax.broadcasted_iota(jnp.int32, (1, OWN * SUF), 1)
    k_row, slot = slot >> 6, slot & (SUF - 1)
    live = jnp.zeros(k_row.shape, jnp.int32)
    for j in range(OWN):
        live = jnp.where(k_row == j, jnp.broadcast_to(lives[j], live.shape), live)
    masks = []
    for source in sources:
        first = ((source * N_YHI + yhi) * N_CORE + core) * SUF
        masks.append(q_row == jnp.where(slot + first < live, k_row, -1))

    b_scores = [score(q_sel[:PICKED], key(kv, COM, BRA)) for kv in kvs[:-1]]
    s_scores = [score(q_sel[PICKED:], key(kv, *suffix), mask) for kv, mask in zip(kvs[:-1], masks)]
    own_load.wait()
    scores.append(score(q, key(own, 0, COM)))
    b_scores.append(score(q_sel[:PICKED], key(own, COM, BRA)))
    s_scores.append(score(q_sel[PICKED:], key(own, *suffix), masks[-1]))
    out, top, total = weigh(scores, values(0, COM))
    b_out, b_top, b_total = weigh(b_scores, values(COM, BRA))
    s_out, s_top, s_total = weigh(s_scores, values(*suffix), masks)

    square = (2 * PICKED, 4 * PICKED)
    column = lax.broadcasted_iota(jnp.int32, square, 1)
    eye = lax.broadcasted_iota(jnp.int32, square, 0) == column & (2 * PICKED - 1)

    def across(a, b):
        col = jnp.broadcast_to(jnp.concatenate([a, b], axis=0), square)
        return jnp.sum(jnp.where(eye, col, 0.0), axis=0, keepdims=True)

    shape = (LINES, 4 * PICKED)
    place_of = lax.broadcasted_iota(jnp.int32, shape, 0) == picked_lines(picks, 1)
    first = lax.broadcasted_iota(jnp.int32, shape, 1) < 2 * PICKED
    p_top = jnp.where(place_of, jnp.broadcast_to(across(b_top, s_top), shape), LOW)
    high = jnp.maximum(top, jnp.max(p_top, axis=1, keepdims=True))
    weight = jnp.where(place_of, jnp.exp2(p_top - high), 0.0)
    scale = jnp.exp2(top - high)
    near = weight.astype(BF16).astype(F32)
    weights = [jnp.where(first, near, weight - near), jnp.where(first, near, 0.0)]
    parts = jnp.concatenate([b_out, s_out], axis=0)
    p_near = parts.astype(BF16).astype(F32)
    parts = [p_near, p_near, parts - p_near, jnp.zeros_like(parts)]
    out = out * scale + jnp.dot(
        jnp.concatenate(weights, axis=1).astype(BF16),
        jnp.concatenate(parts, axis=0).astype(BF16),
        preferred_element_type=F32,
    )
    weight = jnp.where(first, weight, 0.0)
    total = total * scale + jnp.sum(weight * across(b_total, s_total), axis=1, keepdims=True)

    power = jnp.ceil(jnp.log(jnp.max(jnp.abs(out), axis=1, keepdims=True)) * math.log2(math.e))
    power = jnp.clip(power, -120.0, 120.0)
    out = out * jnp.exp2(-power)
    tile = (1, 8, HEAD_DIM)
    lane = lax.broadcasted_iota(jnp.int32, tile, 2)
    lane = lane - (lax.broadcasted_iota(jnp.int32, tile, 1) & (OWN - 1))
    shape = (LINES // 8, 8, HEAD_DIM)

    def lanes_of(at, value):
        value = jnp.broadcast_to(value, (LINES, HEAD_DIM)).reshape(shape)
        return jnp.where(jnp.broadcast_to(lane == at, shape), value, 0.0)

    stat = lanes_of(POWER_AT, power)
    for value, lanes in ((high, TOP_AT), (total, TOTAL_AT)):
        for at in lanes:
            piece = value.astype(BF16).astype(F32)
            stat = stat + lanes_of(at, piece)
            value = value - piece
    stat = stat.reshape(LINES, HEAD_DIM)
    stat = stat + pltpu.roll(stat, 1, 0)
    stat = stat + pltpu.roll(stat, 2, 0)
    for c in range(PEERS):
        out_ref[pl.ds(c * CHUNK, OWN)] = out[c * OWN : (c + 1) * OWN]
        out_ref[pl.ds(c * CHUNK + OWN, 2)] = stat[(c + 1) * OWN - 2 : (c + 1) * OWN]


def merge_kernel(parts, out):
    stat = parts[pl.ds(CHUNK - 1, PEERS, stride=CHUNK), :]

    def value(*lanes):
        return sum(pltpu.roll(stat, (HEAD_DIM - at) % HEAD_DIM, 1) for at in lanes)

    top = value(*TOP_AT)
    high = jnp.max(top, axis=0, keepdims=True)
    weight = jnp.exp2(jnp.minimum(top - high, 0.0))
    total = jnp.sum(weight * value(*TOTAL_AT), axis=0, keepdims=True)
    weight = weight * jnp.exp2(value(POWER_AT))
    rows = []
    for r in range(OWN):
        part = parts[pl.ds(r, PEERS, stride=CHUNK), :]
        got = jnp.sum(part * weight[:, r : r + 1], axis=0, keepdims=True)
        rows.append(got / total[:, r : r + 1])
    out[...] = jnp.concatenate(rows, axis=0).astype(BF16)


def call(kernel, outs, specs, scratch=(), out_specs=None, limit=VMEM_LIMIT):
    return pl.pallas_call(
        kernel,
        out_shape=outs,
        in_specs=specs,
        out_specs=out_specs or jax.tree.map(lambda _: VMEM, outs),
        scratch_shapes=scratch,
        compiler_params=pltpu.CompilerParams(vmem_limit_bytes=limit),
    )


def turn(value, axis, step):
    size = lax.axis_size(axis)
    return lax.ppermute(value, axis, [(i, (i + step) % size) for i in range(size)])


def local(
    queries,
    row_branch,
    suffix_len,
    common_keys,
    common_values,
    branch_keys,
    branch_values,
    suffix_keys,
    suffix_values,
):
    width = KV_HEADS * HEAD_DIM
    flat = [
        a.reshape(-1, width)
        for a in (common_keys, common_values, branch_keys, branch_values, suffix_keys, suffix_values)
    ]
    block = (2 * KEYS, HEAD_DIM)
    block = (2 * KEYS, HEAD_DIM)
    q, *packed = call(
        pack_kernel,
        [
            jax.ShapeDtypeStruct((PEERS, OWN, HEAD_DIM), BF16),
            jax.ShapeDtypeStruct((OWN_ROOM, HEAD_DIM), BF16),
        ]
        + [jax.ShapeDtypeStruct(block, BF16)] * (N_X - 1),
        [HBM] * 9,
        [
            pltpu.VMEM((2 * KEYS, width), BF16),
            pltpu.VMEM((N_X, *block), BF16),
            pltpu.VMEM((INFO, HEAD_DIM), BF16),
            pltpu.VMEM((1, OWN, HEAD_DIM), BF16),
            pltpu.VMEM((PEERS, OWN, HEAD_DIM), BF16),
            pltpu.SMEM((ROWS,), jnp.int32),
            pltpu.SMEM((OWN,), jnp.int32),
            pltpu.SMEM((2 * OWN,), jnp.int32),
            pltpu.SemaphoreType.DMA((9,)),
            pltpu.SemaphoreType.DMA((N_X, 7)),
        ],
        [HBM] * (1 + N_X),
        PACK_LIMIT,
    )(queries[None], row_branch, suffix_len, *flat)
    kvs = [turn(packed[i], "x", i) for i in STEPS]

    q = lax.all_to_all(q, PLANE, split_axis=0, concat_axis=0, tiled=True)
    q = q.reshape(LINES, HEAD_DIM)
    parts = call(
        attend_kernel,
        jax.ShapeDtypeStruct((PEERS * CHUNK, HEAD_DIM), F32),
        [HBM] + [VMEM] * 4,
        [
            pltpu.VMEM(block, BF16),
            pltpu.VMEM((INFO, HEAD_DIM), BF16),
            pltpu.SemaphoreType.DMA((2,)),
        ],
    )(packed[0], q, *kvs)
    parts = parts.astype(jnp.float16).reshape(PEERS * CHUNK // 2, 2, HEAD_DIM)
    parts = lax.all_to_all(parts, PLANE, split_axis=0, concat_axis=0, tiled=True)
    parts = parts.reshape(PEERS * CHUNK, HEAD_DIM).astype(F32)
    return call(merge_kernel, jax.ShapeDtypeStruct((OWN, HEAD_DIM), BF16), [VMEM])(parts)


def solution(mesh):
    axes = ("ylo", "z", "x", "yhi", "core")
    fine = Mesh(mesh.devices.reshape(N_YLO, N_Z, N_X, N_YHI, N_CORE), axes)
    branch, seq = ("ylo", "z"), ("x", "yhi", "core")
    return jax.shard_map(
        local,
        mesh=fine,
        in_specs=(
            P(branch, seq),
            P(),
            P(branch),
            P(branch + seq, None),
            P(branch + seq, None),
            P(branch, seq, None),
            P(branch, seq, None),
            P(branch, seq, None),
            P(branch, seq, None),
        ),
        out_specs=P(branch, seq),
        check_vma=False,
    )
```
